512 devices in a mesh: grp: 16 (over z, core), rd: 32 (over y, x).
Axes of the slice: x: 4, y: 8, z: 8, core: 2. Of those that a mesh axis runs over, the one named last changes fastest.
Arguments:
- leaf_rows: float32 [32, 4096, 256], P('grp', 'rd'), may hold values from -0.46403883 to 0.46403883
- leaf_inverse: float32 [32, 256, 256], P('grp'), as said below
- block_pattern: int32 [32, 16], P('grp'), may hold values 0 or 1
- leaf_widths: int32 [32], P('grp'), may hold values from 128 to 256, as said below
- separator: float32 [4096, 4096], P('grp', 'rd'), as said below
Outputs:
- leaf_panels: bfloat16 [32, 4096, 256], P('grp', 'rd')
- level_panel: bfloat16 [256, 4096], P(None, 'rd')
- schur_next: float32 [4096, 4096], P('grp', 'rd')
The draws below stay inside these ranges and needn't reach their ends.
Inputs may be any that keep to these rules, and one draw needn't show every extreme that they name: leaf_inverse[j] is lower triangular with a positive diagonal. `leaf_widths`: some leaf has width 256. `separator`: symmetric and positive definite.
All inputs are finite; a program needn't handle non-finite values. No bound on the sum of `block_pattern` on one device may be relied on, other than what follows from the above.
Results may differ from the reference program's by a relative error of at most 0.013.
Values may be sent and summed in bfloat16 or wider, within the bound.
No kernel may reach another device: no remote copies, remote signals or barrier semaphores. Data moves between devices by JAX's collectives and lax.ppermute only.
A program may use at most 64 MiB of HBM per device.

```python
import jax
import jax.numpy as jnp
from jax import lax

B = 256
ROWS_RD = 128
LEAVES = 32
SEP = 4096
SEP_BLOCKS = 16


def draw_leaf_rows(key, part):
    key = jax.random.fold_in(key, 4)
    noise_key, pair_key = jax.random.split(key, 2)
    base_scale = 2.0 / (LEAVES * B) ** 0.5
    values = jnp.clip(jax.random.normal(noise_key, (LEAVES, SEP, B), jnp.float32), -4.5, 4.5)
    leaf_scale = jnp.ones((LEAVES,), jnp.float32)
    paired = jax.random.randint(pair_key, (LEAVES,), 0, SEP // ROWS_RD)
    rows = jnp.arange(SEP, dtype=jnp.int32)
    boosted = (rows[None, :] // ROWS_RD == paired[:, None]) & (rows[None, :] >= B)
    factor_rows = jnp.where(boosted, 3.0, 1.0) * leaf_scale[:, None]
    return values * factor_rows[:, :, None] * base_scale


def draw_leaf_widths(key, part):
    key = jax.random.fold_in(key, 1)
    widths = jax.random.randint(key, (LEAVES,), B // 2, B + 1)
    chosen = jax.random.randint(jax.random.fold_in(key, 2), (), 0, LEAVES)
    return widths.at[chosen].set(B).astype(jnp.int32)


def draw_leaf_inverse(key, part):
    key = jax.random.fold_in(key, 2)
    diag_key, off_key = jax.random.split(key)
    diagonal = jax.random.uniform(diag_key, (LEAVES, B), jnp.float32, 0.6, 1.4)
    lower_part = jax.random.normal(off_key, (LEAVES, B, B), jnp.float32)
    lower_part = lower_part * (0.6 / B ** 0.5)
    strict = jnp.tril(jnp.ones((B, B), jnp.float32), -1)
    identity = jnp.eye(B, dtype=jnp.float32)
    return lower_part * strict[None] + diagonal[:, :, None] * identity[None]


def draw_separator(key, part):
    key = jax.random.fold_in(key, 3)
    noise_key, lead_key, tail_key, size_key, sign_key, weight_key = jax.random.split(key, 6)
    raw_draw = jax.random.normal(noise_key, (SEP, SEP), jnp.float32)
    symmetric = (raw_draw + raw_draw.T) * 0.7071
    indices = jnp.arange(SEP, dtype=jnp.int32)
    leading = indices < B
    both_lead = leading[:, None] & leading[None, :]
    both_tail = (~leading)[:, None] & (~leading)[None, :]
    spread = jnp.where(both_lead, 3.4 / B ** 0.5, jnp.where(both_tail, 0.005, 0.5 / (SEP - B) ** 0.5))
    lead_diag = jax.random.uniform(lead_key, (SEP,), jnp.float32, 15.0, 19.0)
    tail_diag = jax.random.uniform(tail_key, (SEP,), jnp.float32, 8.0, 12.0)
    diag_values = jnp.where(leading, lead_diag, tail_diag)
    magnitude = jax.random.uniform(size_key, (SEP,), jnp.float32, 0.6, 1.4)
    sign_values = jnp.where(jax.random.bernoulli(sign_key, 0.5, (SEP,)), 1.0, -1.0)
    coupling = jnp.where(leading, 0.0, magnitude * sign_values) * (80.0 * B / (1.0533 * (SEP - B))) ** 0.5
    classes = indices % B
    weights = jax.random.uniform(weight_key, (B,), jnp.float32, 0.4, 0.6)
    linked = (classes[None, :] == indices[:, None]) & leading[:, None]
    crossing = jnp.where(linked, coupling[None, :], 0.0)
    same_class = (classes[:, None] == classes[None, :]) & both_tail
    class_weight = weights[classes]
    tail_block = jnp.where(same_class, coupling[:, None] * coupling[None, :] * class_weight[:, None], 0.0)
    return symmetric * spread + crossing + crossing.T + tail_block + jnp.diag(diag_values)


def set_ends(result, rng, smallest, top_value):
    longest = result.shape.index(max(result.shape))
    spots = []
    for shift in (0, 1):
        where = [jax.random.randint(jax.random.fold_in(rng, axis), (), 0, length) for axis, length in enumerate(result.shape)]
        where[longest] = (where[longest] + shift) % result.shape[longest]
        spots.append(tuple(where))
    return result.at[spots[0]].set(smallest).at[spots[1]].set(top_value)


def setup_inputs(seed: int = 0) -> dict:
    seeds = jax.random.split(jax.random.key(seed), 6)
    leaf_rows = draw_leaf_rows(jax.random.fold_in(seeds[5], 71), 0)
    leaf_inverse = draw_leaf_inverse(jax.random.fold_in(seeds[5], 71), 0)
    block_pattern = set_ends((jax.random.randint(seeds[2], (LEAVES, SEP_BLOCKS), 0, 2) < 1).astype(jnp.int32), jax.random.fold_in(seeds[2], 1), 0, 1)
    leaf_widths = draw_leaf_widths(jax.random.fold_in(seeds[5], 71), 0)
    separator = draw_separator(jax.random.fold_in(seeds[5], 71), 0)
    return dict(leaf_rows=leaf_rows, leaf_inverse=leaf_inverse, block_pattern=block_pattern, leaf_widths=leaf_widths, separator=separator)


def reference(leaf_rows, leaf_inverse, block_pattern, leaf_widths, separator):
    product = jnp.einsum('jib,jcb->jic', leaf_rows, leaf_inverse, precision=lax.Precision.HIGHEST)
    row_ids = jnp.arange(SEP, dtype=jnp.int32) // B
    row_mask = block_pattern[:, row_ids].astype(jnp.float32)
    col_mask = (jnp.arange(B, dtype=jnp.int32)[None, :] < leaf_widths[:, None]).astype(jnp.float32)
    panels = (product * row_mask[:, :, None] * col_mask[:, None, :]).astype(jnp.bfloat16)
    wide = panels.astype(jnp.float32)
    update = jnp.einsum('jkc,jic->ki', wide, wide)
    schur = separator - update
    factor = jnp.linalg.cholesky(schur[:B, :B])
    level = jax.scipy.linalg.solve_triangular(factor, schur[:B, :], lower=True).astype(jnp.bfloat16)
    outer = jnp.dot(level.T.astype(jnp.float32), level.astype(jnp.float32), preferred_element_type=jnp.float32)
    ids = jnp.arange(SEP, dtype=jnp.int32)
    keep = (ids[:, None] >= B) & (ids[None, :] >= B)
    schur_next = jnp.where(keep, schur - outer, jnp.float32(0.0))
    return (panels, level, schur_next)
```

```python
import jax
import jax.numpy as jnp
from jax import lax
from jax.sharding import Mesh, PartitionSpec as P

Z, C, Y, X = 8, 2, 8, 4
HI = lax.Precision.HIGHEST
F32 = jnp.float32
BF16 = jnp.bfloat16


def dot_t(a, b, out=F32):
    return lax.dot_general(a, b, (((1,), (1,)), ((), ())), preferred_element_type=out)


def share(array, axis, size):
    copies = jnp.broadcast_to(array[None], (size,) + array.shape)
    return lax.all_to_all(copies, axis, 0, 0, tiled=True)


def body(leaf_rows, leaf_inverse, block_pattern, leaf_widths, separator):
    count, rows, width = leaf_rows.shape
    z, c, y, x = (lax.axis_index(a) for a in ("z", "c", "y", "x"))
    even = x % 2 == 0

    lead = lax.all_gather(separator, "y", axis=0)[0]

    product = jnp.einsum("jib,jcb->jic", leaf_rows, leaf_inverse, precision=HI)
    row_mask = lax.dynamic_slice_in_dim(block_pattern, 2 * y + x // 2, 1, 1).astype(F32)
    col_mask = (jnp.arange(width, dtype=jnp.int32)[None, :] < leaf_widths[:, None]).astype(F32)
    panels = (product * row_mask[:, :, None] * col_mask[:, None, :]).astype(BF16)
    own = jnp.concatenate([panels[j] for j in range(count)], axis=1)
    depth = own.shape[1]

    along_y = share(own, "y", Y)
    along_x = share(jnp.stack([own, along_y[0]]), "x", X)
    along_x = along_x.reshape(X, 2, rows, depth)
    first = along_x[:2, 1].reshape(2 * rows, depth)
    row_blocks = along_y.reshape(Y * rows, depth)
    col_blocks = along_x[:, 0].reshape(X * rows, depth)

    half = 2 * rows
    theirs = lax.dynamic_slice_in_dim(col_blocks, (1 - c) * half, half, 0)
    mine = lax.dynamic_slice_in_dim(col_blocks, c * half, half, 0)
    sent = lax.ppermute(dot_t(row_blocks, theirs).astype(BF16), "c", [(0, 1), (1, 0)])
    terms = (dot_t(row_blocks, mine) + sent.astype(F32)).astype(BF16)
    update = lax.psum_scatter(terms, "z", scatter_dimension=0, tiled=True)

    one = lax.ppermute(lead, "x", [(0, 1), (1, 0)])
    two = lax.ppermute(lead, "x", [(0, 2), (1, 3)])
    three = lax.ppermute(lead, "x", [(0, 3), (1, 2)])
    lead0 = jnp.where(x == 0, lead, jnp.where(x == 1, one, jnp.where(x == 2, two, three)))
    lead1 = jnp.where(x == 1, lead, jnp.where(x == 0, one, jnp.where(x == 3, two, three)))
    base = jnp.concatenate([lead0, lead1, separator], axis=1)
    base = jnp.where((z == 0) & (c == 0), base, jnp.zeros_like(base))
    part = base - dot_t(first, jnp.concatenate([first, own], axis=0))
    pieces = lax.all_to_all(part.reshape(Z * C, width // (Z * C), 3 * rows), ("z", "c"), 0, 0, tiled=True)
    top = lax.all_gather(jnp.sum(pieces, axis=0), ("z", "c"), axis=0, tiled=True)
    top_own = top[:, width:]

    def flip(t):
        pairs = []
        for zs in range(Z):
            for cs in range(C):
                for ys in range(Y):
                    for xs in range(X):
                        src = ((zs * C + cs) * Y + ys) * X + xs
                        dst = ((ys * C + xs // 2) * Y + zs) * X + 2 * cs + ((xs % 2) ^ t)
                        pairs.append((src, dst))
        return lax.ppermute(top_own, ("z", "c", "y", "x"), pairs)

    straight, crossed = flip(0), flip(1)
    top_rows = jnp.concatenate(
        [jnp.where(even, straight, crossed), jnp.where(even, crossed, straight)], axis=1
    )

    lead_block = top[:, :width]
    factor = jnp.linalg.cholesky((lead_block + lead_block.T) * 0.5)
    level = jax.scipy.linalg.solve_triangular(
        factor, jnp.concatenate([top_own, top_rows], axis=1), lower=True
    ).astype(BF16)
    level_own = level[:, :rows]
    level_rows = level[:, rows:]

    def place(t):
        pairs = []
        for cs in range(C):
            for xs in range(X):
                pairs.append((cs * X + xs, (xs // 2) * X + 2 * cs + ((xs % 2) ^ t)))
        which = (x % 2) ^ t
        block = lax.dynamic_slice_in_dim(update, which * rows, rows, 1)
        return lax.ppermute(block, ("c", "x"), pairs)

    near, far = place(0), place(1)
    update_own = jnp.concatenate(
        [jnp.where(even, near, far), jnp.where(even, far, near)], axis=0
    ).astype(F32)

    schur = separator - update_own
    outer = lax.dot_general(
        level_rows, level_own, (((0,), (0,)), ((), ())), preferred_element_type=F32
    )
    keep = ((z > 0) | (c > 0)) & ((y > 0) | (x > 1))
    schur_next = jnp.where(keep, schur - outer, jnp.float32(0.0))
    return (panels, level_own, schur_next)


def solution(mesh):
    fine = Mesh(mesh.devices.reshape(Z, C, Y, X), ("z", "c", "y", "x"))
    grp, rd = ("z", "c"), ("y", "x")
    return jax.shard_map(
        body,
        mesh=fine,
        in_specs=(
            P(grp, rd, None),
            P(grp, None, None),
            P(grp, None),
            P(grp),
            P(grp, rd),
        ),
        out_specs=(P(grp, rd, None), P(None, rd), P(grp, rd)),
        check_vma=False,
    )
```

```python
import jax
import jax.numpy as jnp
from jax import lax
from jax.experimental import pallas as pl
from jax.experimental.pallas import tpu as pltpu
from jax.sharding import Mesh, PartitionSpec as P

Z, C, Y, X = 8, 2, 8, 4
HI = lax.Precision.HIGHEST
F32 = jnp.float32
BF16 = jnp.bfloat16
BLOCK, LANES, SUB = 64, 128, 8


def dot_t(a, b, out=F32):
    return lax.dot_general(a, b, (((1,), (1,)), ((), ())), preferred_element_type=out)


def share(array, axis, size):
    copies = jnp.broadcast_to(array[None], (size,) + array.shape)
    return lax.all_to_all(copies, axis, 0, 0, tiled=True)


def lane(tile, k):
    return jnp.broadcast_to(tile[:, k:k + 1], tile.shape)

def sub(tile, s):
    return jnp.broadcast_to(tile[s:s + 1, :], tile.shape)

def block_inverse(block):
    n = BLOCK
    rowid = lax.broadcasted_iota(jnp.int32, (SUB, LANES), 0)
    laneid = lax.broadcasted_iota(jnp.int32, (SUB, LANES), 1)
    wide = jnp.concatenate([block, jnp.zeros((n, LANES - n), F32)], axis=1)
    tiles = []
    for t in range(n // SUB):
        unit = jnp.where(laneid == rowid + (n + t * SUB), 1.0, 0.0).astype(F32)
        tiles.append(wide[t * SUB:(t + 1) * SUB, :] + unit)
    out = [None] * len(tiles)
    for t in range(len(tiles)):
        acc = jnp.zeros((SUB, LANES), F32)
        for s in range(0, SUB, 2):
            k = t * SUB + s
            r1, r2 = sub(tiles[t], s), sub(tiles[t], s + 1)
            a, b, d = lane(r1, k), lane(r1, k + 1), lane(r2, k + 1)
            inv = 1.0 / (a * d - b * b)
            q1 = (d * r1 - b * r2) * inv
            q2 = (a * r2 - b * r1) * inv
            for u in range(t, len(tiles)):
                c1, c2 = lane(tiles[u], k), lane(tiles[u], k + 1)
                new = tiles[u] - (c1 * q1 + c2 * q2)
                tiles[u] = jnp.where(rowid > s + 1, new, tiles[u]) if u == t else new
            ratio = b / a
            acc = jnp.where(rowid == s, r1 * lax.rsqrt(a), acc)
            acc = jnp.where(rowid == s + 1, (r2 - ratio * r1) * lax.rsqrt(d - ratio * b), acc)
        out[t] = acc
    return jnp.concatenate(out, axis=0)[:, n:]

def kernel(a_ref, w_ref, aug):
    n = a_ref.shape[0]
    a = a_ref[...]
    a = a * 0.5 + a.T * 0.5
    ri = lax.broadcasted_iota(jnp.int32, (n, n), 0)
    ci = lax.broadcasted_iota(jnp.int32, (n, n), 1)
    diag = jnp.where(ri == ci, a, 0.0)
    s_row = lax.rsqrt(jnp.sum(diag, axis=0, keepdims=True))
    s_col = lax.rsqrt(jnp.sum(diag, axis=1, keepdims=True))
    aug[:, :n] = a * s_col * s_row
    aug[:, n:] = jnp.where(ri == ci, 1.0, 0.0)
    for k in range(0, n, BLOCK):
        rows = aug[k:k + BLOCK, :]
        inv = block_inverse(rows[:, k:k + BLOCK])
        u = jnp.dot(inv, rows, precision=HI, preferred_element_type=F32)
        w_ref[k:k + BLOCK, :] = u[:, n:] * s_row
        for m in range(k + BLOCK, n, BLOCK):
            aug[m:m + BLOCK, :] = aug[m:m + BLOCK, :] - lax.dot_general(
                u[:, m:m + BLOCK], u, (((0,), (0,)), ((), ())), precision=HI, preferred_element_type=F32)

def inverse_factor(a):
    n=a.shape[0]
    return pl.pallas_call(kernel, out_shape=jax.ShapeDtypeStruct((n,n),F32),
        in_specs=[pl.BlockSpec(memory_space=pltpu.VMEM)], out_specs=pl.BlockSpec(memory_space=pltpu.VMEM),
        scratch_shapes=[pltpu.VMEM((n,2*n),F32)],
        compiler_params=pltpu.CompilerParams(vmem_limit_bytes=32 * 1024 * 1024),
        name="inverse_factor",
    )(a)


def body(leaf_rows, leaf_inverse, block_pattern, leaf_widths, separator):
    count, rows, width = leaf_rows.shape
    z, c, y, x = (lax.axis_index(a) for a in ("z", "c", "y", "x"))
    even = x % 2 == 0

    slab = width // (Z * C)
    base_own = lax.all_to_all(separator, ("z", "c"), 0, 0, tiled=True)[:slab]
    lead = share(base_own, ("y", "x"), Y * X)
    base = jnp.concatenate([lead[0], lead[1], base_own], axis=1)

    product = jnp.einsum("jib,jcb->jic", leaf_rows, leaf_inverse, precision=HI)
    row_mask = lax.dynamic_slice_in_dim(block_pattern, 2 * y + x // 2, 1, 1).astype(F32)
    col_mask = (jnp.arange(width, dtype=jnp.int32)[None, :] < leaf_widths[:, None]).astype(F32)
    panels = (product * row_mask[:, :, None] * col_mask[:, None, :]).astype(BF16)
    own = jnp.concatenate([panels[j] for j in range(count)], axis=1)
    depth = own.shape[1]

    along_y = share(own, "y", Y)
    along_x = share(jnp.stack([own, along_y[0]]), "x", X)
    along_x = along_x.reshape(X, 2, rows, depth)
    first = along_x[:2, 1].reshape(2 * rows, depth)
    row_blocks = along_y.reshape(Y * rows, depth)
    col_blocks = along_x[:, 0].reshape(X * rows, depth)

    half = 2 * rows
    theirs = lax.dynamic_slice_in_dim(col_blocks, (1 - c) * half, half, 0)
    mine = lax.dynamic_slice_in_dim(col_blocks, c * half, half, 0)
    sent = lax.ppermute(dot_t(row_blocks, theirs).astype(BF16), "c", [(0, 1), (1, 0)])
    terms = (dot_t(row_blocks, mine) + sent.astype(F32)).astype(BF16)

    part = dot_t(first, jnp.concatenate([first, own], axis=0))
    pieces = lax.all_to_all(part.reshape(Z * C, slab, 3 * rows), ("z", "c"), 0, 0, tiled=True)
    top, terms = lax.optimization_barrier((base - jnp.sum(pieces, axis=0), terms))
    terms = lax.all_to_all(terms.reshape(Z, rows, half), "z", 0, 0, tiled=True)
    update = jnp.sum(terms.astype(F32), axis=0)
    top = lax.all_gather(top, ("z", "c"), axis=0, tiled=True)
    top_own = top[:, width:]

    def flip(t):
        pairs = []
        for zs in range(Z):
            for cs in range(C):
                for ys in range(Y):
                    for xs in range(X):
                        src = ((zs * C + cs) * Y + ys) * X + xs
                        dst = ((ys * C + xs // 2) * Y + zs) * X + 2 * cs + ((xs % 2) ^ t)
                        pairs.append((src, dst))
        return lax.ppermute(top_own, ("z", "c", "y", "x"), pairs)

    straight, crossed = flip(0), flip(1)
    top_rows = jnp.concatenate(
        [jnp.where(even, straight, crossed), jnp.where(even, crossed, straight)], axis=1
    )

    inverse = inverse_factor(top[:, :width])
    level = jnp.dot(inverse, jnp.concatenate([top_own, top_rows], axis=1), precision=HI).astype(BF16)
    level_own = level[:, :rows]
    level_rows = level[:, rows:]

    def place(t):
        pairs = []
        for cs in range(C):
            for xs in range(X):
                pairs.append((cs * X + xs, (xs // 2) * X + 2 * cs + ((xs % 2) ^ t)))
        which = (x % 2) ^ t
        block = lax.dynamic_slice_in_dim(update, which * rows, rows, 1)
        return lax.ppermute(block, ("c", "x"), pairs)

    near, far = place(0), place(1)
    update_own = jnp.concatenate(
        [jnp.where(even, near, far), jnp.where(even, far, near)], axis=0
    )

    schur = separator - update_own
    outer = lax.dot_general(
        level_rows, level_own, (((0,), (0,)), ((), ())), preferred_element_type=F32
    )
    keep = ((z > 0) | (c > 0)) & ((y > 0) | (x > 1))
    schur_next = jnp.where(keep, schur - outer, jnp.float32(0.0))
    return (panels, level_own, schur_next)


def solution(mesh):
    fine = Mesh(mesh.devices.reshape(Z, C, Y, X), ("z", "c", "y", "x"))
    grp, rd = ("z", "c"), ("y", "x")
    return jax.shard_map(
        body,
        mesh=fine,
        in_specs=(
            P(grp, rd, None),
            P(grp, None, None),
            P(grp, None),
            P(grp),
            P(grp, rd),
        ),
        out_specs=(P(grp, rd, None), P(None, rd), P(grp, rd)),
        check_vma=False,
    )
```

```python
import jax
import jax.numpy as jnp
from jax import lax
from jax.experimental import pallas as pl
from jax.experimental.pallas import tpu as pltpu
from jax.sharding import Mesh, PartitionSpec as P

Z, C, Y, X = 8, 2, 8, 4
HI = lax.Precision.HIGHEST
F32 = jnp.float32
BF16 = jnp.bfloat16
BLOCK, LANES, SUB = 64, 128, 8


def dot_t(a, b, out=F32):
    return lax.dot_general(a, b, (((1,), (1,)), ((), ())), preferred_element_type=out)


def share(array, axis, size):
    copies = jnp.broadcast_to(array[None], (size,) + array.shape)
    return lax.all_to_all(copies, axis, 0, 0, tiled=True)


def lane(tile, k):
    return jnp.broadcast_to(tile[:, k:k + 1], tile.shape)

def sub(tile, s):
    return jnp.broadcast_to(tile[s:s + 1, :], tile.shape)

def block_inverse(block):
    n = BLOCK
    rowid = lax.broadcasted_iota(jnp.int32, (SUB, LANES), 0)
    laneid = lax.broadcasted_iota(jnp.int32, (SUB, LANES), 1)
    wide = jnp.concatenate([block, jnp.zeros((n, LANES - n), F32)], axis=1)
    tiles = []
    for t in range(n // SUB):
        unit = jnp.where(laneid == rowid + (n + t * SUB), 1.0, 0.0).astype(F32)
        tiles.append(wide[t * SUB:(t + 1) * SUB, :] + unit)
    out = [None] * len(tiles)
    for t in range(len(tiles)):
        acc = jnp.zeros((SUB, LANES), F32)
        for s in range(0, SUB, 2):
            k = t * SUB + s
            r1, r2 = sub(tiles[t], s), sub(tiles[t], s + 1)
            a, b, d = lane(r1, k), lane(r1, k + 1), lane(r2, k + 1)
            inv = 1.0 / (a * d - b * b)
            q1 = (d * r1 - b * r2) * inv
            q2 = (a * r2 - b * r1) * inv
            for u in range(t, len(tiles)):
                c1, c2 = lane(tiles[u], k), lane(tiles[u], k + 1)
                new = tiles[u] - (c1 * q1 + c2 * q2)
                tiles[u] = jnp.where(rowid > s + 1, new, tiles[u]) if u == t else new
            ratio = b / a
            acc = jnp.where(rowid == s, r1 * lax.rsqrt(a), acc)
            acc = jnp.where(rowid == s + 1, (r2 - ratio * r1) * lax.rsqrt(d - ratio * b), acc)
        out[t] = acc
    return jnp.concatenate(out, axis=0)[:, n:]

def eliminate(aug, w_ref, s_row, start):
    n = aug.shape[1] // 2
    count = aug.shape[0]
    for k in range(0, w_ref.shape[0], BLOCK):
        rows = aug[k:k + BLOCK, :]
        inv = block_inverse(rows[:, start + k:start + k + BLOCK])
        u = jnp.dot(inv, rows, precision=HI, preferred_element_type=F32)
        w_ref[k:k + BLOCK, :] = u[:, n:] * s_row
        for m in range(k + BLOCK, count, BLOCK):
            left = u[:, start + m:start + m + BLOCK]
            aug[m:m + BLOCK, :] = aug[m:m + BLOCK, :] - lax.dot_general(
                left, u, (((0,), (0,)), ((), ())), precision=HI, preferred_element_type=F32
            )


def first_half(a_ref, w_ref, rest_ref, scale_ref, aug):
    n = a_ref.shape[0]
    a = a_ref[...]
    a = a * 0.5 + a.T * 0.5
    ri = lax.broadcasted_iota(jnp.int32, (n, n), 0)
    ci = lax.broadcasted_iota(jnp.int32, (n, n), 1)
    diag = jnp.where(ri == ci, a, 0.0)
    s_row = lax.rsqrt(jnp.sum(diag, axis=0, keepdims=True))
    s_col = lax.rsqrt(jnp.sum(diag, axis=1, keepdims=True))
    aug[:, :n] = a * s_col * s_row
    aug[:, n:] = jnp.where(ri == ci, 1.0, 0.0)
    eliminate(aug, w_ref, s_row, 0)
    rest_ref[...] = aug[n // 2:, :]
    scale_ref[...] = jnp.broadcast_to(s_row, scale_ref.shape)


def second_half(rest_ref, scale_ref, w_ref, aug):
    aug[...] = rest_ref[...]
    eliminate(aug, w_ref, scale_ref[:1, :], rest_ref.shape[0])


def in_vmem(body, outs, scratch, name, *args):
    spec = pl.BlockSpec(memory_space=pltpu.VMEM)
    return pl.pallas_call(
        body,
        out_shape=[jax.ShapeDtypeStruct(shape, F32) for shape in outs],
        in_specs=[spec] * len(args),
        out_specs=[spec] * len(outs),
        scratch_shapes=[pltpu.VMEM(scratch, F32)],
        compiler_params=pltpu.CompilerParams(vmem_limit_bytes=32 * 1024 * 1024),
        cost_estimate=pl.CostEstimate(flops=10**10, bytes_accessed=10**6, transcendentals=0),
        name=name,
    )(*args)


def body(leaf_rows, leaf_inverse, block_pattern, leaf_widths, separator):
    count, rows, width = leaf_rows.shape
    z, c, y, x = (lax.axis_index(a) for a in ("z", "c", "y", "x"))
    even = x % 2 == 0

    def move(array, steps):
        pairs = [(X * ys + xs, X * yd + xd) for (ys, xs), (yd, xd) in steps]
        return lax.ppermute(array, ("z", "c", "y", "x"), pairs)

    lead = separator
    for span in (4, 2, 1):
        steps = [((ys, xs), (ys + span, xs)) for ys in range(0, Y, 2 * span) for xs in range(2)]
        lead = jnp.where(y % (2 * span) == span, move(lead, steps), lead)
    steps = [((ys, xs), (ys, xs + 2)) for ys in range(Y) for xs in range(2)]
    lead = jnp.where(x >= 2, move(lead, steps), lead)
    steps = [((ys, xs), (ys, xs ^ 1)) for ys in range(Y) for xs in range(X)]
    beside = move(lead, steps)
    base = jnp.concatenate([jnp.where(even, lead, beside), jnp.where(even, beside, lead), separator], axis=1)
    base = jnp.where((z == 0) & (c == 0), base, jnp.zeros_like(base))

    product = jnp.einsum("jib,jcb->jic", leaf_rows, leaf_inverse, precision=HI)
    row_mask = lax.dynamic_slice_in_dim(block_pattern, 2 * y + x // 2, 1, 1).astype(F32)
    col_mask = (jnp.arange(width, dtype=jnp.int32)[None, :] < leaf_widths[:, None]).astype(F32)
    panels = (product * row_mask[:, :, None] * col_mask[:, None, :]).astype(BF16)
    own = jnp.concatenate([panels[j] for j in range(count)], axis=1)
    depth = own.shape[1]

    along_y = share(own, "y", Y)
    along_x = share(jnp.stack([own, along_y[0]]), "x", X)
    along_x = along_x.reshape(X, 2, rows, depth)
    first = along_x[:2, 1].reshape(2 * rows, depth)
    row_blocks = along_y.reshape(Y * rows, depth)
    col_blocks = along_x[:, 0].reshape(X * rows, depth)

    half = 2 * rows
    theirs = lax.dynamic_slice_in_dim(col_blocks, (1 - c) * half, half, 0)
    mine = lax.dynamic_slice_in_dim(col_blocks, c * half, half, 0)
    sent = lax.ppermute(dot_t(row_blocks, theirs).astype(BF16), "c", [(0, 1), (1, 0)])
    terms = (dot_t(row_blocks, mine) + sent.astype(F32)).astype(BF16)

    update = lax.psum_scatter(terms, "z", scatter_dimension=0, tiled=True)

    slab = width // (Z * C)
    part = base - dot_t(first, jnp.concatenate([first, own], axis=0))
    pieces = lax.all_to_all(part.reshape(Z * C, slab, 3 * rows), ("z", "c"), 0, 0, tiled=True)
    top = lax.all_gather(jnp.sum(pieces, axis=0), ("z", "c"), axis=0, tiled=True)
    top_own = top[:, width:]

    half_rows = width // 2
    upper, rest, scale = in_vmem(
        first_half, [(half_rows, width), (half_rows, 2 * width), (SUB, width)], (width, 2 * width),
        "first_half", top[:, :width],
    )
    rest, top_own, update = lax.optimization_barrier((rest, top_own, update))
    (lower,) = in_vmem(
        second_half, [(half_rows, width)], (half_rows, 2 * width), "second_half", rest, scale
    )
    inverse = jnp.concatenate([upper, lower], axis=0)

    def flip(t):
        pairs = []
        for zs in range(Z):
            for cs in range(C):
                for ys in range(Y):
                    for xs in range(X):
                        src = ((zs * C + cs) * Y + ys) * X + xs
                        dst = ((ys * C + xs // 2) * Y + zs) * X + 2 * cs + ((xs % 2) ^ t)
                        pairs.append((src, dst))
        return lax.ppermute(top_own, ("z", "c", "y", "x"), pairs)

    straight, crossed = flip(0), flip(1)
    top_rows = jnp.concatenate(
        [jnp.where(even, straight, crossed), jnp.where(even, crossed, straight)], axis=1
    )

    level = jnp.dot(inverse, jnp.concatenate([top_own, top_rows], axis=1), precision=HI).astype(BF16)
    level_own = level[:, :rows]
    level_rows = level[:, rows:]

    def place(t):
        pairs = []
        for cs in range(C):
            for xs in range(X):
                pairs.append((cs * X + xs, (xs // 2) * X + 2 * cs + ((xs % 2) ^ t)))
        which = (x % 2) ^ t
        block = lax.dynamic_slice_in_dim(update, which * rows, rows, 1)
        return lax.ppermute(block, ("c", "x"), pairs)

    near, far = place(0), place(1)
    update_own = jnp.concatenate(
        [jnp.where(even, near, far), jnp.where(even, far, near)], axis=0
    ).astype(F32)

    schur = separator - update_own
    outer = lax.dot_general(
        level_rows, level_own, (((0,), (0,)), ((), ())), preferred_element_type=F32
    )
    keep = ((z > 0) | (c > 0)) & ((y > 0) | (x > 1))
    schur_next = jnp.where(keep, schur - outer, jnp.float32(0.0))
    return (panels, level_own, schur_next)


def solution(mesh):
    fine = Mesh(mesh.devices.reshape(Z, C, Y, X), ("z", "c", "y", "x"))
    grp, rd = ("z", "c"), ("y", "x")
    return jax.shard_map(
        body,
        mesh=fine,
        in_specs=(
            P(grp, rd, None),
            P(grp, None, None),
            P(grp, None),
            P(grp),
            P(grp, rd),
        ),
        out_specs=(P(grp, rd, None), P(None, rd), P(grp, rd)),
        check_vma=False,
    )
```

```python
import jax
import jax.numpy as jnp
from jax import lax
from jax.experimental import pallas as pl
from jax.experimental.pallas import tpu as pltpu
from jax.sharding import Mesh, PartitionSpec as P

Z, C, Y, X = 8, 2, 8, 4
HI = lax.Precision.HIGHEST
F32 = jnp.float32
BF16 = jnp.bfloat16
BLOCK, LANES, SUB = 64, 128, 8


def dot_t(a, b, out=F32):
    return lax.dot_general(a, b, (((1,), (1,)), ((), ())), preferred_element_type=out)


def share(array, axis, size):
    copies = jnp.broadcast_to(array[None], (size,) + array.shape)
    return lax.all_to_all(copies, axis, 0, 0, tiled=True)


def lane(tile, k):
    return jnp.broadcast_to(tile[:, k:k + 1], tile.shape)

def sub(tile, s):
    return jnp.broadcast_to(tile[s:s + 1, :], tile.shape)

def group_rows(tile, start):
    r = [sub(tile, s) for s in range(SUB)]
    d = [[lane(r[i], start + j) if j >= i else None for j in range(SUB)] for i in range(SUB)]
    pairs = []
    for p in range(0, SUB, 2):
        a, b, e = d[p][p], d[p][p + 1], d[p + 1][p + 1]
        inv = 1.0 / (a * e - b * b)
        ia, ib, ie = a * inv, b * inv, e * inv
        raw, low = {}, {}
        for i in range(p + 2, SUB):
            raw[i] = (e * d[p][i] - b * d[p + 1][i], a * d[p + 1][i] - b * d[p][i])
        for i in range(p + 2, SUB):
            for j in range(i, SUB):
                d[i][j] = d[i][j] - inv * (raw[i][0] * d[p][j] + raw[i][1] * d[p + 1][j])
            low[i] = (raw[i][0] * inv, raw[i][1] * inv)
            r[i] = r[i] - (low[i][0] * r[p] + low[i][1] * r[p + 1])
        pairs.append((a, b, e, ia, ib, ie, low))
    solved = [None] * SUB
    for p in range(SUB - 2, -1, -2):
        a, b, e, ia, ib, ie, low = pairs[p // 2]
        s0 = ie * r[p] - ib * r[p + 1]
        s1 = ia * r[p + 1] - ib * r[p]
        for i in range(p + 2, SUB):
            s0 = s0 - low[i][0] * solved[i]
            s1 = s1 - low[i][1] * solved[i]
        solved[p], solved[p + 1] = s0, s1
    norm = [None] * SUB
    for p in range(0, SUB, 2):
        a, b, e = pairs[p // 2][:3]
        ratio = b / a
        norm[p] = r[p] * lax.rsqrt(a)
        norm[p + 1] = (r[p + 1] - ratio * r[p]) * lax.rsqrt(e - ratio * b)
    return norm, solved

def block_inverse(block):
    n = BLOCK
    rowid = lax.broadcasted_iota(jnp.int32, (SUB, LANES), 0)
    laneid = lax.broadcasted_iota(jnp.int32, (SUB, LANES), 1)
    wide = jnp.concatenate([block, jnp.zeros((n, LANES - n), F32)], axis=1)
    tiles = []
    for t in range(n // SUB):
        unit = jnp.where(laneid == rowid + (n + t * SUB), 1.0, 0.0).astype(F32)
        tiles.append(wide[t * SUB:(t + 1) * SUB, :] + unit)
    for t in range(len(tiles)):
        norm, solved = group_rows(tiles[t], t * SUB)
        for u in range(t + 1, len(tiles)):
            terms = [lane(tiles[u], t * SUB + s) * solved[s] for s in range(SUB)]
            while len(terms) > 1:
                terms = [x + y for x, y in zip(terms[::2], terms[1::2])]
            tiles[u] = tiles[u] - terms[0]
        out = norm[0]
        for s in range(1, SUB):
            out = jnp.where(rowid == s, norm[s], out)
        tiles[t] = out
    return jnp.concatenate(tiles, axis=0)[:, n:]


def eliminate(aug, w_ref, s_row, start):
    n = aug.shape[1] // 2
    count = aug.shape[0]
    for k in range(0, w_ref.shape[0], BLOCK):
        rows = aug[k:k + BLOCK, :]
        inv = block_inverse(rows[:, start + k:start + k + BLOCK])
        u = jnp.dot(inv, rows, precision=HI, preferred_element_type=F32)
        w_ref[k:k + BLOCK, :] = u[:, n:] * s_row
        for m in range(k + BLOCK, count, BLOCK):
            left = u[:, start + m:start + m + BLOCK]
            aug[m:m + BLOCK, :] = aug[m:m + BLOCK, :] - lax.dot_general(
                left, u, (((0,), (0,)), ((), ())), precision=HI, preferred_element_type=F32
            )


def first_half(a_ref, w_ref, rest_ref, scale_ref, aug):
    n = a_ref.shape[0]
    a = a_ref[...]
    a = a * 0.5 + a.T * 0.5
    ri = lax.broadcasted_iota(jnp.int32, (n, n), 0)
    ci = lax.broadcasted_iota(jnp.int32, (n, n), 1)
    diag = jnp.where(ri == ci, a, 0.0)
    s_row = lax.rsqrt(jnp.sum(diag, axis=0, keepdims=True))
    s_col = lax.rsqrt(jnp.sum(diag, axis=1, keepdims=True))
    aug[:, :n] = a * s_col * s_row
    aug[:, n:] = jnp.where(ri == ci, 1.0, 0.0)
    eliminate(aug, w_ref, s_row, 0)
    rest_ref[...] = aug[n // 2:, :]
    scale_ref[...] = jnp.broadcast_to(s_row, scale_ref.shape)


def second_half(rest_ref, scale_ref, w_ref, aug):
    aug[...] = rest_ref[...]
    eliminate(aug, w_ref, scale_ref[:1, :], rest_ref.shape[0])


def in_vmem(body, outs, scratch, name, *args):
    spec = pl.BlockSpec(memory_space=pltpu.VMEM)
    return pl.pallas_call(
        body,
        out_shape=[jax.ShapeDtypeStruct(shape, F32) for shape in outs],
        in_specs=[spec] * len(args),
        out_specs=[spec] * len(outs),
        scratch_shapes=[pltpu.VMEM(scratch, F32)],
        compiler_params=pltpu.CompilerParams(vmem_limit_bytes=32 * 1024 * 1024),
        cost_estimate=pl.CostEstimate(flops=10**10, bytes_accessed=10**6, transcendentals=0),
        name=name,
    )(*args)


def body(leaf_rows, leaf_inverse, block_pattern, leaf_widths, separator):
    count, rows, width = leaf_rows.shape
    z, c, y, x = (lax.axis_index(a) for a in ("z", "c", "y", "x"))
    even = x % 2 == 0

    product = jnp.einsum("jib,jcb->jic", leaf_rows, leaf_inverse, precision=HI)
    row_mask = lax.dynamic_slice_in_dim(block_pattern, 2 * y + x // 2, 1, 1).astype(F32)
    col_mask = (jnp.arange(width, dtype=jnp.int32)[None, :] < leaf_widths[:, None]).astype(F32)
    panels = (product * row_mask[:, :, None] * col_mask[:, None, :]).astype(BF16)
    own = jnp.concatenate([panels[j] for j in range(count)], axis=1)
    depth = own.shape[1]

    shifted = [own] + [lax.ppermute(own, "x", [(i, (i + k) % X) for i in range(X)]) for k in range(1, X)]

    def move(array, steps):
        pairs = [(X * ys + xs, X * yd + xd) for (ys, xs), (yd, xd) in steps]
        return lax.ppermute(array, ("z", "c", "y", "x"), pairs)

    lead, *shifted = lax.optimization_barrier((separator, *shifted))
    for span in (4, 2, 1):
        steps = [((ys, xs), (ys + span, xs)) for ys in range(0, Y, 2 * span) for xs in range(2)]
        lead = jnp.where(y % (2 * span) == span, move(lead, steps), lead)

    def across(*moves):
        return move(lead, [((ys, src), (ys, dst)) for ys in range(Y) for src, dst in moves])

    one, two, three = across((0, 1), (1, 0)), across((0, 2), (1, 3)), across((0, 3), (1, 2))
    lead0 = jnp.where(x == 0, lead, jnp.where(x == 1, one, jnp.where(x == 2, two, three)))
    lead1 = jnp.where(x == 1, lead, jnp.where(x == 0, one, jnp.where(x == 3, two, three)))
    base = jnp.concatenate([lead0, lead1, separator], axis=1)
    base = jnp.where((z == 0) & (c == 0), base, jnp.zeros_like(base))

    along_y = share(own, "y", Y)
    row_blocks = along_y.reshape(Y * rows, depth)
    first = share(along_y[0], "x", X)[:2].reshape(2 * rows, depth)
    def column(place):
        block = shifted[0]
        for k in range(1, X):
            block = jnp.where((x - place) % X == k, shifted[k], block)
        return block

    half = 2 * rows
    theirs = jnp.concatenate([column(2 - 2 * c), column(3 - 2 * c)], axis=0)
    mine = jnp.concatenate([column(2 * c), column(2 * c + 1)], axis=0)
    sent = lax.ppermute(dot_t(row_blocks, theirs).astype(BF16), "c", [(0, 1), (1, 0)])
    terms = (dot_t(row_blocks, mine) + sent.astype(F32)).astype(BF16)

    update = lax.psum_scatter(terms, "z", scatter_dimension=0, tiled=True)

    slab = width // (Z * C)
    part = base - dot_t(first, jnp.concatenate([first, own], axis=0))
    pieces = lax.all_to_all(part.reshape(Z * C, slab, 3 * rows), ("z", "c"), 0, 0, tiled=True)
    top = lax.all_gather(jnp.sum(pieces, axis=0), ("z", "c"), axis=0, tiled=True)
    top_own = top[:, width:]

    half_rows = width // 2
    upper, rest, scale = in_vmem(
        first_half, [(half_rows, width), (half_rows, 2 * width), (SUB, width)], (width, 2 * width),
        "first_half", top[:, :width],
    )
    rest, top_own, update = lax.optimization_barrier((rest, top_own, update))
    (lower,) = in_vmem(
        second_half, [(half_rows, width)], (half_rows, 2 * width), "second_half", rest, scale
    )
    inverse = jnp.concatenate([upper, lower], axis=0)

    def flip(t):
        pairs = []
        for zs in range(Z):
            for cs in range(C):
                for ys in range(Y):
                    for xs in range(X):
                        src = ((zs * C + cs) * Y + ys) * X + xs
                        dst = ((ys * C + xs // 2) * Y + zs) * X + 2 * cs + ((xs % 2) ^ t)
                        pairs.append((src, dst))
        return lax.ppermute(top_own, ("z", "c", "y", "x"), pairs)

    straight, crossed = flip(0), flip(1)
    top_rows = jnp.concatenate(
        [jnp.where(even, straight, crossed), jnp.where(even, crossed, straight)], axis=1
    )

    level = jnp.dot(inverse, jnp.concatenate([top_own, top_rows], axis=1), precision=HI).astype(BF16)
    level_own = level[:, :rows]
    level_rows = level[:, rows:]

    def place(t):
        pairs = []
        for cs in range(C):
            for xs in range(X):
                pairs.append((cs * X + xs, (xs // 2) * X + 2 * cs + ((xs % 2) ^ t)))
        which = (x % 2) ^ t
        block = lax.dynamic_slice_in_dim(update, which * rows, rows, 1)
        return lax.ppermute(block, ("c", "x"), pairs)

    near, far = place(0), place(1)
    update_own = jnp.concatenate(
        [jnp.where(even, near, far), jnp.where(even, far, near)], axis=0
    ).astype(F32)

    schur = separator - update_own
    outer = lax.dot_general(
        level_rows, level_own, (((0,), (0,)), ((), ())), preferred_element_type=F32
    )
    keep = ((z > 0) | (c > 0)) & ((y > 0) | (x > 1))
    schur_next = jnp.where(keep, schur - outer, jnp.float32(0.0))
    return (panels, level_own, schur_next)


def solution(mesh):
    fine = Mesh(mesh.devices.reshape(Z, C, Y, X), ("z", "c", "y", "x"))
    grp, rd = ("z", "c"), ("y", "x")
    return jax.shard_map(
        body,
        mesh=fine,
        in_specs=(
            P(grp, rd, None),
            P(grp, None, None),
            P(grp, None),
            P(grp),
            P(grp, rd),
        ),
        out_specs=(P(grp, rd, None), P(None, rd), P(grp, rd)),
        check_vma=False,
    )
```

```python
import jax
import jax.numpy as jnp
from jax import lax
from jax.experimental import pallas as pl
from jax.experimental.pallas import tpu as pltpu
from jax.sharding import Mesh, PartitionSpec as P

Z, C, Y, X = 8, 2, 8, 4
HI = lax.Precision.HIGHEST
F32 = jnp.float32
BF16 = jnp.bfloat16
BLOCK, LANES, SUB = 64, 128, 8


def dot_t(a, b, out=F32):
    return lax.dot_general(a, b, (((1,), (1,)), ((), ())), preferred_element_type=out)


def share(array, axis, size):
    copies = jnp.broadcast_to(array[None], (size,) + array.shape)
    return lax.all_to_all(copies, axis, 0, 0, tiled=True)


def lane(tile, k):
    return jnp.broadcast_to(tile[:, k:k + 1], tile.shape)

def sub(tile, s):
    return jnp.broadcast_to(tile[s:s + 1, :], tile.shape)

def group_rows(tile, start):
    r = [sub(tile, s) for s in range(SUB)]
    d = [[lane(r[i], start + j) if j >= i else None for j in range(SUB)] for i in range(SUB)]
    pairs = []
    for p in range(0, SUB, 2):
        a, b, e = d[p][p], d[p][p + 1], d[p + 1][p + 1]
        inv = 1.0 / (a * e - b * b)
        ia, ib, ie = a * inv, b * inv, e * inv
        raw, low = {}, {}
        for i in range(p + 2, SUB):
            raw[i] = (e * d[p][i] - b * d[p + 1][i], a * d[p + 1][i] - b * d[p][i])
        for i in range(p + 2, SUB):
            for j in range(i, SUB):
                d[i][j] = d[i][j] - inv * (raw[i][0] * d[p][j] + raw[i][1] * d[p + 1][j])
            low[i] = (raw[i][0] * inv, raw[i][1] * inv)
            r[i] = r[i] - (low[i][0] * r[p] + low[i][1] * r[p + 1])
        pairs.append((a, b, e, ia, ib, ie, low))
    solved = [None] * SUB
    for p in range(SUB - 2, -1, -2):
        a, b, e, ia, ib, ie, low = pairs[p // 2]
        s0 = ie * r[p] - ib * r[p + 1]
        s1 = ia * r[p + 1] - ib * r[p]
        for i in range(p + 2, SUB):
            s0 = s0 - low[i][0] * solved[i]
            s1 = s1 - low[i][1] * solved[i]
        solved[p], solved[p + 1] = s0, s1
    norm = [None] * SUB
    for p in range(0, SUB, 2):
        a, b, e = pairs[p // 2][:3]
        ratio = b / a
        norm[p] = r[p] * lax.rsqrt(a)
        norm[p + 1] = (r[p + 1] - ratio * r[p]) * lax.rsqrt(e - ratio * b)
    return norm, solved

def block_inverse(block):
    n = BLOCK
    rowid = lax.broadcasted_iota(jnp.int32, (SUB, LANES), 0)
    laneid = lax.broadcasted_iota(jnp.int32, (SUB, LANES), 1)
    wide = jnp.concatenate([block, jnp.zeros((n, LANES - n), F32)], axis=1)
    tiles = []
    for t in range(n // SUB):
        unit = jnp.where(laneid == rowid + (n + t * SUB), 1.0, 0.0).astype(F32)
        tiles.append(wide[t * SUB:(t + 1) * SUB, :] + unit)
    for t in range(len(tiles)):
        norm, solved = group_rows(tiles[t], t * SUB)
        for u in range(t + 1, len(tiles)):
            terms = [lane(tiles[u], t * SUB + s) * solved[s] for s in range(SUB)]
            while len(terms) > 1:
                terms = [x + y for x, y in zip(terms[::2], terms[1::2])]
            tiles[u] = tiles[u] - terms[0]
        out = norm[0]
        for s in range(1, SUB):
            out = jnp.where(rowid == s, norm[s], out)
        tiles[t] = out
    return jnp.concatenate(tiles, axis=0)[:, n:]


def eliminate(aug, w_ref, s_row, start):
    n = aug.shape[1] // 2
    count = aug.shape[0]
    for k in range(0, w_ref.shape[0], BLOCK):
        rows = aug[k:k + BLOCK, :]
        inv = block_inverse(rows[:, start + k:start + k + BLOCK])
        u = jnp.dot(inv, rows, precision=HI, preferred_element_type=F32)
        w_ref[k:k + BLOCK, :] = u[:, n:] * s_row
        for m in range(k + BLOCK, count, BLOCK):
            left = u[:, start + m:start + m + BLOCK]
            aug[m:m + BLOCK, :] = aug[m:m + BLOCK, :] - lax.dot_general(
                left, u, (((0,), (0,)), ((), ())), precision=HI, preferred_element_type=F32
            )


def inverse_factor(a_ref, w_ref, aug):
    n = a_ref.shape[0]
    a = a_ref[:, :n]
    a = a * 0.5 + a.T * 0.5
    ri = lax.broadcasted_iota(jnp.int32, (n, n), 0)
    ci = lax.broadcasted_iota(jnp.int32, (n, n), 1)
    diag = jnp.where(ri == ci, a, 0.0)
    s_row = lax.rsqrt(jnp.sum(diag, axis=0, keepdims=True))
    s_col = lax.rsqrt(jnp.sum(diag, axis=1, keepdims=True))
    aug[:, :n] = a * s_col * s_row
    aug[:, n:] = jnp.where(ri == ci, 1.0, 0.0)
    eliminate(aug, w_ref, s_row, 0)


def in_vmem(body, outs, scratch, name, *args):
    spec = pl.BlockSpec(memory_space=pltpu.VMEM)
    return pl.pallas_call(
        body,
        out_shape=[jax.ShapeDtypeStruct(shape, F32) for shape in outs],
        in_specs=[spec] * len(args),
        out_specs=[spec] * len(outs),
        scratch_shapes=[pltpu.VMEM(scratch, F32)],
        compiler_params=pltpu.CompilerParams(vmem_limit_bytes=32 * 1024 * 1024),
        cost_estimate=pl.CostEstimate(flops=10**10, bytes_accessed=10**6, transcendentals=0),
        name=name,
    )(*args)


def body(leaf_rows, leaf_inverse, block_pattern, leaf_widths, separator):
    count, rows, width = leaf_rows.shape
    z, c, y, x = (lax.axis_index(a) for a in ("z", "c", "y", "x"))
    even = x % 2 == 0

    product = jnp.einsum("jib,jcb->jic", leaf_rows, leaf_inverse, precision=HI)
    row_mask = lax.dynamic_slice_in_dim(block_pattern, 2 * y + x // 2, 1, 1).astype(F32)
    col_mask = (jnp.arange(width, dtype=jnp.int32)[None, :] < leaf_widths[:, None]).astype(F32)
    panels = (product * row_mask[:, :, None] * col_mask[:, None, :]).astype(BF16)
    own = jnp.concatenate([panels[j] for j in range(count)], axis=1)
    depth = own.shape[1]

    def send(array, pairs):
        return lax.ppermute(array, ("y", "x"), [(X * ys + xs, X * yd + xd) for (ys, xs), (yd, xd) in pairs])

    block = own
    for k in range(1, Y):
        got = send(own, [((0, xs), (k, xs)) for xs in range(2)])
        block = jnp.where(y == k, got, block)
    own, block = lax.optimization_barrier((own, block))
    one, two, three = (
        send(block, [((ys, src), (ys, dst)) for ys in range(Y) for src, dst in moves])
        for moves in (((0, 1), (1, 0)), ((0, 2), (1, 3)), ((0, 3), (1, 2)))
    )
    first = jnp.concatenate(
        [
            jnp.where(x == 0, block, jnp.where(x == 1, one, jnp.where(x == 2, two, three))),
            jnp.where(x == 1, block, jnp.where(x == 0, one, jnp.where(x == 3, two, three))),
        ],
        axis=0,
    )
    along_y = share(own, "y", Y)
    shifted = [lax.ppermute(own, "x", [(i, (i + k) % X) for i in range(X)]) for k in range(1, X)]

    slab = width // (Z * C)
    base = jnp.where((z == 0) & (c == 0), separator, jnp.zeros_like(separator))
    part = base - dot_t(first, own)
    part, along_y, *shifted = lax.optimization_barrier((part, along_y, *shifted))
    pieces = lax.all_to_all(part.reshape(Z * C, slab, rows), ("z", "c"), 0, 0, tiled=True)
    strip = jnp.sum(pieces, axis=0)

    shifted = [own] + shifted
    cols = []
    for k in range(X):
        place = (2 * c + x % 2) ^ k
        found = shifted[0]
        for m in range(1, X):
            found = jnp.where((x - place) % X == m, shifted[m], found)
        cols.append(found)
    terms = dot_t(along_y.reshape(Y * rows, depth), jnp.concatenate(cols, axis=0)).astype(BF16)
    moved = []
    for k in range(X):
        pairs = [(cs * X + xs, (xs // 2) * X + ((2 * cs + xs % 2) ^ k)) for cs in range(C) for xs in range(X)]
        moved.append(lax.ppermute(terms[:, k * rows:(k + 1) * rows], ("c", "x"), pairs).astype(F32))
    upper, lower = (moved[0] + moved[2]).astype(BF16), (moved[1] + moved[3]).astype(BF16)
    terms = jnp.stack([jnp.where(even, upper, lower), jnp.where(even, lower, upper)])
    terms = terms.reshape(2, Z, rows, rows).transpose(1, 0, 2, 3).reshape(Z, width, rows)

    strips = share(strip, ("y", "x"), Y * X)
    lead = jnp.concatenate([strips[0], strips[1], strip], axis=1)
    groups = strips.reshape(Z * C, 2, slab, rows).transpose(0, 2, 1, 3).reshape(Z * C, slab, width)
    top = jnp.concatenate([jnp.broadcast_to(lead[None], (Z * C,) + lead.shape), groups], axis=2)
    top, terms = lax.optimization_barrier((top, terms))
    top = lax.all_to_all(top, ("z", "c"), 0, 0, tiled=True).reshape(width, 5 * rows)
    top, terms = lax.optimization_barrier((top, terms))
    top_own, top_rows = top[:, width:width + rows], top[:, width + rows:]
    update = jnp.sum(lax.all_to_all(terms, "z", 0, 0, tiled=True).astype(F32), axis=0)

    (inverse,) = in_vmem(inverse_factor, [(width, width)], (width, 2 * width), "inverse_factor", top[:, :width])
    level = jnp.dot(inverse, jnp.concatenate([top_own, top_rows], axis=1), precision=HI).astype(BF16)
    level_own = level[:, :rows]
    level_rows = level[:, rows:]

    schur = separator - update
    outer = lax.dot_general(
        level_rows, level_own, (((0,), (0,)), ((), ())), preferred_element_type=F32
    )
    keep = ((z > 0) | (c > 0)) & ((y > 0) | (x > 1))
    schur_next = jnp.where(keep, schur - outer, jnp.float32(0.0))
    return (panels, level_own, schur_next)


def solution(mesh):
    fine = Mesh(mesh.devices.reshape(Z, C, Y, X), ("z", "c", "y", "x"))
    grp, rd = ("z", "c"), ("y", "x")
    return jax.shard_map(
        body,
        mesh=fine,
        in_specs=(
            P(grp, rd, None),
            P(grp, None, None),
            P(grp, None),
            P(grp),
            P(grp, rd),
        ),
        out_specs=(P(grp, rd, None), P(None, rd), P(grp, rd)),
        check_vma=False,
    )
```

```python
import jax
import jax.numpy as jnp
from jax import lax
from jax.experimental import pallas as pl
from jax.experimental.pallas import tpu as pltpu
from jax.sharding import Mesh, PartitionSpec as P

Z, C, Y, X = 8, 2, 8, 4
HI = lax.Precision.HIGHEST
F32 = jnp.float32
BF16 = jnp.bfloat16
BLOCK, LANES, SUB = 64, 128, 8


def dot_t(a, b, out=F32):
    return lax.dot_general(a, b, (((1,), (1,)), ((), ())), preferred_element_type=out)


def share(array, axis, size):
    copies = jnp.broadcast_to(array[None], (size,) + array.shape)
    return lax.all_to_all(copies, axis, 0, 0, tiled=True)


def lane(tile, k):
    return jnp.broadcast_to(tile[:, k:k + 1], tile.shape)

def sub(tile, s):
    return jnp.broadcast_to(tile[s:s + 1, :], tile.shape)

def group_rows(tile, start):
    r = [sub(tile, s) for s in range(SUB)]
    d = [[lane(r[i], start + j) if j >= i else None for j in range(SUB)] for i in range(SUB)]
    pairs = []
    for p in range(0, SUB, 2):
        a, b, e = d[p][p], d[p][p + 1], d[p + 1][p + 1]
        inv = 1.0 / (a * e - b * b)
        ia, ib, ie = a * inv, b * inv, e * inv
        raw, low = {}, {}
        for i in range(p + 2, SUB):
            raw[i] = (e * d[p][i] - b * d[p + 1][i], a * d[p + 1][i] - b * d[p][i])
        for i in range(p + 2, SUB):
            for j in range(i, SUB):
                d[i][j] = d[i][j] - inv * (raw[i][0] * d[p][j] + raw[i][1] * d[p + 1][j])
            low[i] = (raw[i][0] * inv, raw[i][1] * inv)
            r[i] = r[i] - (low[i][0] * r[p] + low[i][1] * r[p + 1])
        pairs.append((a, b, e, ia, ib, ie, low))
    solved = [None] * SUB
    for p in range(SUB - 2, -1, -2):
        a, b, e, ia, ib, ie, low = pairs[p // 2]
        s0 = ie * r[p] - ib * r[p + 1]
        s1 = ia * r[p + 1] - ib * r[p]
        for i in range(p + 2, SUB):
            s0 = s0 - low[i][0] * solved[i]
            s1 = s1 - low[i][1] * solved[i]
        solved[p], solved[p + 1] = s0, s1
    norm = [None] * SUB
    for p in range(0, SUB, 2):
        a, b, e = pairs[p // 2][:3]
        ratio = b / a
        norm[p] = r[p] * lax.rsqrt(a)
        norm[p + 1] = (r[p + 1] - ratio * r[p]) * lax.rsqrt(e - ratio * b)
    return norm, solved

def block_inverse(block):
    n = BLOCK
    rowid = lax.broadcasted_iota(jnp.int32, (SUB, LANES), 0)
    laneid = lax.broadcasted_iota(jnp.int32, (SUB, LANES), 1)
    wide = jnp.concatenate([block, jnp.zeros((n, LANES - n), F32)], axis=1)
    tiles = []
    for t in range(n // SUB):
        unit = jnp.where(laneid == rowid + (n + t * SUB), 1.0, 0.0).astype(F32)
        tiles.append(wide[t * SUB:(t + 1) * SUB, :] + unit)
    for t in range(len(tiles)):
        norm, solved = group_rows(tiles[t], t * SUB)
        for u in range(t + 1, len(tiles)):
            terms = [lane(tiles[u], t * SUB + s) * solved[s] for s in range(SUB)]
            while len(terms) > 1:
                terms = [x + y for x, y in zip(terms[::2], terms[1::2])]
            tiles[u] = tiles[u] - terms[0]
        out = norm[0]
        for s in range(1, SUB):
            out = jnp.where(rowid == s, norm[s], out)
        tiles[t] = out
    return jnp.concatenate(tiles, axis=0)[:, n:]


def eliminate(aug, w_ref, s_row, start):
    n = aug.shape[1] // 2
    count = aug.shape[0]
    for k in range(0, w_ref.shape[0], BLOCK):
        rows = aug[k:k + BLOCK, :]
        inv = block_inverse(rows[:, start + k:start + k + BLOCK])
        u = jnp.dot(inv, rows, precision=HI, preferred_element_type=F32)
        w_ref[k:k + BLOCK, :] = u[:, n:] * s_row
        for m in range(k + BLOCK, count, BLOCK):
            left = u[:, start + m:start + m + BLOCK]
            aug[m:m + BLOCK, :] = aug[m:m + BLOCK, :] - lax.dot_general(
                left, u, (((0,), (0,)), ((), ())), precision=HI, preferred_element_type=F32
            )


def inverse_factor(a_ref, w_ref, aug):
    n = a_ref.shape[0]
    a = a_ref[:, :n]
    a = a * 0.5 + a.T * 0.5
    ri = lax.broadcasted_iota(jnp.int32, (n, n), 0)
    ci = lax.broadcasted_iota(jnp.int32, (n, n), 1)
    diag = jnp.where(ri == ci, a, 0.0)
    s_row = lax.rsqrt(jnp.sum(diag, axis=0, keepdims=True))
    s_col = lax.rsqrt(jnp.sum(diag, axis=1, keepdims=True))
    aug[:, :n] = a * s_col * s_row
    aug[:, n:] = jnp.where(ri == ci, 1.0, 0.0)
    eliminate(aug, w_ref, s_row, 0)


def in_vmem(body, outs, scratch, name, *args):
    spec = pl.BlockSpec(memory_space=pltpu.VMEM)
    return pl.pallas_call(
        body,
        out_shape=[jax.ShapeDtypeStruct(shape, F32) for shape in outs],
        in_specs=[spec] * len(args),
        out_specs=[spec] * len(outs),
        scratch_shapes=[pltpu.VMEM(scratch, F32)],
        compiler_params=pltpu.CompilerParams(vmem_limit_bytes=32 * 1024 * 1024),
        cost_estimate=pl.CostEstimate(flops=10**10, bytes_accessed=10**6, transcendentals=0),
        name=name,
    )(*args)


def body(leaf_rows, leaf_inverse, block_pattern, leaf_widths, separator):
    count, rows, width = leaf_rows.shape
    z, c, y, x = (lax.axis_index(a) for a in ("z", "c", "y", "x"))
    even = x % 2 == 0

    product = jnp.einsum("jib,jcb->jic", leaf_rows, leaf_inverse, precision=HI)
    row_mask = lax.dynamic_slice_in_dim(block_pattern, 2 * y + x // 2, 1, 1).astype(F32)
    col_mask = (jnp.arange(width, dtype=jnp.int32)[None, :] < leaf_widths[:, None]).astype(F32)
    panels = (product * row_mask[:, :, None] * col_mask[:, None, :]).astype(BF16)
    own = jnp.concatenate([panels[j] for j in range(count)], axis=1)
    depth = own.shape[1]

    def send(array, pairs):
        return lax.ppermute(array, ("y", "x"), [(X * ys + xs, X * yd + xd) for (ys, xs), (yd, xd) in pairs])

    along_y = share(own, "y", Y)
    block = along_y[0]
    shifted = [lax.ppermute(own, "x", [(i, (i + k) % X) for i in range(X)]) for k in range(1, X)]
    block, *shifted = lax.optimization_barrier((block, *shifted))
    one, two, three = (
        send(block, [((ys, src), (ys, dst)) for ys in range(Y) for src, dst in moves])
        for moves in (((0, 1), (1, 0)), ((0, 2), (1, 3)), ((0, 3), (1, 2)))
    )
    first = jnp.concatenate(
        [
            jnp.where(x == 0, block, jnp.where(x == 1, one, jnp.where(x == 2, two, three))),
            jnp.where(x == 1, block, jnp.where(x == 0, one, jnp.where(x == 3, two, three))),
        ],
        axis=0,
    )
    slab = width // (Z * C)
    base = jnp.where((z == 0) & (c == 0), separator, jnp.zeros_like(separator))
    part = base - dot_t(first, own)
    pieces = lax.all_to_all(part.reshape(Z * C, slab, rows), ("z", "c"), 0, 0, tiled=True)
    strip = jnp.sum(pieces, axis=0)

    strips = share(strip, ("y", "x"), Y * X)

    shifted = [own] + shifted
    cols = []
    for k in range(X):
        place = (2 * c + x % 2) ^ k
        found = shifted[0]
        for m in range(1, X):
            found = jnp.where((x - place) % X == m, shifted[m], found)
        cols.append(found)
    terms = dot_t(along_y.reshape(Y * rows, depth), jnp.concatenate(cols, axis=0)).astype(BF16)
    strips, terms = lax.optimization_barrier((strips, terms))
    moved = []
    for k in range(X):
        pairs = [(cs * X + xs, (xs // 2) * X + ((2 * cs + xs % 2) ^ k)) for cs in range(C) for xs in range(X)]
        moved.append(lax.ppermute(terms[:, k * rows:(k + 1) * rows], ("c", "x"), pairs).astype(F32))
    upper, lower = (moved[0] + moved[2]).astype(BF16), (moved[1] + moved[3]).astype(BF16)
    terms = jnp.stack([jnp.where(even, upper, lower), jnp.where(even, lower, upper)])
    terms = terms.reshape(2, Z, rows, rows).transpose(1, 0, 2, 3).reshape(Z, width, rows)

    lead = jnp.concatenate([strips[0], strips[1], strip], axis=1)
    groups = strips.reshape(Z * C, 2, slab, rows).transpose(0, 2, 1, 3).reshape(Z * C, slab, width)
    top = jnp.concatenate([jnp.broadcast_to(lead[None], (Z * C,) + lead.shape), groups], axis=2)
    top = lax.all_to_all(top, ("z", "c"), 0, 0, tiled=True).reshape(width, 5 * rows)
    top, terms = lax.optimization_barrier((top, terms))
    top_own, top_rows = top[:, width:width + rows], top[:, width + rows:]
    update = jnp.sum(lax.all_to_all(terms, "z", 0, 0, tiled=True).astype(F32), axis=0)

    (inverse,) = in_vmem(inverse_factor, [(width, width)], (width, 2 * width), "inverse_factor", top[:, :width])
    level = jnp.dot(inverse, jnp.concatenate([top_own, top_rows], axis=1), precision=HI).astype(BF16)
    level_own = level[:, :rows]
    level_rows = level[:, rows:]

    schur = separator - update
    outer = lax.dot_general(
        level_rows, level_own, (((0,), (0,)), ((), ())), preferred_element_type=F32
    )
    keep = ((z > 0) | (c > 0)) & ((y > 0) | (x > 1))
    schur_next = jnp.where(keep, schur - outer, jnp.float32(0.0))
    return (panels, level_own, schur_next)


def solution(mesh):
    fine = Mesh(mesh.devices.reshape(Z, C, Y, X), ("z", "c", "y", "x"))
    grp, rd = ("z", "c"), ("y", "x")
    return jax.shard_map(
        body,
        mesh=fine,
        in_specs=(
            P(grp, rd, None),
            P(grp, None, None),
            P(grp, None),
            P(grp),
            P(grp, rd),
        ),
        out_specs=(P(grp, rd, None), P(None, rd), P(grp, rd)),
        check_vma=False,
    )
```

```python
import jax
import jax.numpy as jnp
from jax import lax
from jax.experimental import pallas as pl
from jax.experimental.pallas import tpu as pltpu
from jax.sharding import Mesh, PartitionSpec as P

Z, C, Y, X = 8, 2, 8, 4
HI = lax.Precision.HIGHEST
F32 = jnp.float32
BF16 = jnp.bfloat16
BLOCK, LANES, SUB = 64, 128, 8


def dot_t(a, b, out=F32):
    return lax.dot_general(a, b, (((1,), (1,)), ((), ())), preferred_element_type=out)


def share(array, axis, size):
    copies = jnp.broadcast_to(array[None], (size,) + array.shape)
    return lax.all_to_all(copies, axis, 0, 0, tiled=True)


def lane(tile, k):
    return jnp.broadcast_to(tile[:, k:k + 1], tile.shape)

def sub(tile, s):
    return jnp.broadcast_to(tile[s:s + 1, :], tile.shape)

def group_rows(tile, start):
    r = [sub(tile, s) for s in range(SUB)]
    d = [[lane(r[i], start + j) if j >= i else None for j in range(SUB)] for i in range(SUB)]
    pairs = []
    for p in range(0, SUB, 2):
        a, b, e = d[p][p], d[p][p + 1], d[p + 1][p + 1]
        inv = 1.0 / (a * e - b * b)
        ia, ib, ie = a * inv, b * inv, e * inv
        raw, low = {}, {}
        for i in range(p + 2, SUB):
            raw[i] = (e * d[p][i] - b * d[p + 1][i], a * d[p + 1][i] - b * d[p][i])
        for i in range(p + 2, SUB):
            for j in range(i, SUB):
                d[i][j] = d[i][j] - inv * (raw[i][0] * d[p][j] + raw[i][1] * d[p + 1][j])
            low[i] = (raw[i][0] * inv, raw[i][1] * inv)
            r[i] = r[i] - (low[i][0] * r[p] + low[i][1] * r[p + 1])
        pairs.append((a, b, e, ia, ib, ie, low))
    solved = [None] * SUB
    for p in range(SUB - 2, -1, -2):
        a, b, e, ia, ib, ie, low = pairs[p // 2]
        s0 = ie * r[p] - ib * r[p + 1]
        s1 = ia * r[p + 1] - ib * r[p]
        for i in range(p + 2, SUB):
            s0 = s0 - low[i][0] * solved[i]
            s1 = s1 - low[i][1] * solved[i]
        solved[p], solved[p + 1] = s0, s1
    norm = [None] * SUB
    for p in range(0, SUB, 2):
        a, b, e = pairs[p // 2][:3]
        ratio = b / a
        norm[p] = r[p] * lax.rsqrt(a)
        norm[p + 1] = (r[p + 1] - ratio * r[p]) * lax.rsqrt(e - ratio * b)
    return norm, solved

def block_inverse(block):
    n = BLOCK
    rowid = lax.broadcasted_iota(jnp.int32, (SUB, LANES), 0)
    laneid = lax.broadcasted_iota(jnp.int32, (SUB, LANES), 1)
    wide = jnp.concatenate([block, jnp.zeros((n, LANES - n), F32)], axis=1)
    tiles = []
    for t in range(n // SUB):
        unit = jnp.where(laneid == rowid + (n + t * SUB), 1.0, 0.0).astype(F32)
        tiles.append(wide[t * SUB:(t + 1) * SUB, :] + unit)
    for t in range(len(tiles)):
        norm, solved = group_rows(tiles[t], t * SUB)
        for u in range(t + 1, len(tiles)):
            terms = [lane(tiles[u], t * SUB + s) * solved[s] for s in range(SUB)]
            while len(terms) > 1:
                terms = [x + y for x, y in zip(terms[::2], terms[1::2])]
            tiles[u] = tiles[u] - terms[0]
        out = norm[0]
        for s in range(1, SUB):
            out = jnp.where(rowid == s, norm[s], out)
        tiles[t] = out
    return jnp.concatenate(tiles, axis=0)[:, n:]


def eliminate(aug, w_ref, s_row, start):
    n = aug.shape[1] // 2
    count = aug.shape[0]
    for k in range(0, w_ref.shape[0], BLOCK):
        rows = aug[k:k + BLOCK, :]
        inv = block_inverse(rows[:, start + k:start + k + BLOCK])
        u = jnp.dot(inv, rows, precision=HI, preferred_element_type=F32)
        w_ref[k:k + BLOCK, :] = u[:, n:] * s_row
        for m in range(k + BLOCK, count, BLOCK):
            left = u[:, start + m:start + m + BLOCK]
            aug[m:m + BLOCK, :] = aug[m:m + BLOCK, :] - lax.dot_general(
                left, u, (((0,), (0,)), ((), ())), precision=HI, preferred_element_type=F32
            )


def inverse_factor(a_ref, w_ref, aug):
    n = a_ref.shape[0]
    a = a_ref[:, :n]
    a = a * 0.5 + a.T * 0.5
    ri = lax.broadcasted_iota(jnp.int32, (n, n), 0)
    ci = lax.broadcasted_iota(jnp.int32, (n, n), 1)
    diag = jnp.where(ri == ci, a, 0.0)
    s_row = lax.rsqrt(jnp.sum(diag, axis=0, keepdims=True))
    s_col = lax.rsqrt(jnp.sum(diag, axis=1, keepdims=True))
    aug[:, :n] = a * s_col * s_row
    aug[:, n:] = jnp.where(ri == ci, 1.0, 0.0)
    eliminate(aug, w_ref, s_row, 0)


def in_vmem(body, outs, scratch, name, *args):
    spec = pl.BlockSpec(memory_space=pltpu.VMEM)
    return pl.pallas_call(
        body,
        out_shape=[jax.ShapeDtypeStruct(shape, F32) for shape in outs],
        in_specs=[spec] * len(args),
        out_specs=[spec] * len(outs),
        scratch_shapes=[pltpu.VMEM(scratch, F32)],
        compiler_params=pltpu.CompilerParams(vmem_limit_bytes=32 * 1024 * 1024),
        cost_estimate=pl.CostEstimate(flops=10**10, bytes_accessed=10**6, transcendentals=0),
        name=name,
    )(*args)


def body(leaf_rows, leaf_inverse, block_pattern, leaf_widths, separator):
    count, rows, width = leaf_rows.shape
    z, c, y, x = (lax.axis_index(a) for a in ("z", "c", "y", "x"))
    even = x % 2 == 0

    product = jnp.einsum("jib,jcb->jic", leaf_rows, leaf_inverse, precision=HI)
    row_mask = lax.dynamic_slice_in_dim(block_pattern, 2 * y + x // 2, 1, 1).astype(F32)
    col_mask = (jnp.arange(width, dtype=jnp.int32)[None, :] < leaf_widths[:, None]).astype(F32)
    panels = (product * row_mask[:, :, None] * col_mask[:, None, :]).astype(BF16)
    own = jnp.concatenate([panels[j] for j in range(count)], axis=1)
    depth = own.shape[1]

    along_y = share(own, "y", Y)
    shifted = [own] + [lax.ppermute(own, "x", [(i, (i + k) % X) for i in range(X)]) for k in range(1, X)]

    def choose(blocks, place):
        found = blocks[0]
        for k in range(1, X):
            found = jnp.where((x - place) % X == k, blocks[k], found)
        return found

    def gather_base(*moves):
        rows_of = separator[:rows], separator[rows:]
        to_lower = jnp.zeros((), bool)
        for src, dst in moves:
            to_lower |= (x == src) & (dst == 1)
        pairs = [(X * ys + src, X * ys + dst) for ys in range(Y) for src, dst in moves]
        return lax.ppermute(jnp.where(to_lower, rows_of[1], rows_of[0]), ("z", "c", "y", "x"), pairs)

    swap, two, three = gather_base((0, 1), (1, 0)), gather_base((2, 0), (3, 1)), gather_base((3, 0), (2, 1))
    mine = jnp.where(even, separator[:rows], separator[rows:])
    base = [
        jnp.where(even, mine, swap),
        jnp.where(even, swap, mine),
        jnp.where(even, two, three),
        jnp.where(even, three, two),
    ]
    base = jnp.concatenate(base, axis=1)
    base = jnp.where((z == 0) & (c == 0) & (x < 2), base, jnp.zeros_like(base))
    block, base, *shifted = lax.optimization_barrier((along_y[0], base, *shifted))
    cols = [choose(shifted, place) for place in range(X)]

    strip_rows = rows // (Z * C)
    part = base - dot_t(block, jnp.concatenate(cols, axis=0))
    pieces = lax.all_to_all(part.reshape(Z * C, strip_rows, X * rows), ("z", "c"), 0, 0, tiled=True)
    strip = jnp.sum(pieces, axis=0)
    strips = share(strip, ("y", "x"), Y * X).reshape(Y, X, strip_rows, X, rows)[:, :2]

    row_blocks = along_y.reshape(Y * rows, depth)
    theirs = jnp.concatenate([choose(shifted, 2 - 2 * c), choose(shifted, 3 - 2 * c)], axis=0)
    mine = jnp.concatenate([choose(shifted, 2 * c), choose(shifted, 2 * c + 1)], axis=0)
    sent = lax.ppermute(dot_t(row_blocks, theirs).astype(BF16), "c", [(0, 1), (1, 0)])
    terms = (dot_t(row_blocks, mine) + sent.astype(F32)).astype(BF16)
    strips, terms = lax.optimization_barrier((strips, terms))

    def place(k):
        pairs = [(cs * X + xs, (xs // 2) * X + 2 * cs + ((xs % 2) ^ k)) for cs in range(C) for xs in range(X)]
        block = jnp.where((x % 2) ^ k == 0, terms[:, :rows], terms[:, rows:])
        return lax.ppermute(block, ("c", "x"), pairs).reshape(Z, rows, rows)

    near, far = place(0), place(1)
    terms = jnp.concatenate([jnp.where(even, near, far), jnp.where(even, far, near)], axis=1)

    wide = strips.transpose(0, 3, 1, 2, 4)
    lead = jnp.concatenate([wide[0, 0], wide[0, 1], wide[y, x]], axis=2)
    lead = jnp.broadcast_to(lead[None], (Z * C,) + lead.shape)
    wide = wide.reshape(Z * C, 2, 2, strip_rows, rows)
    top = jnp.concatenate([lead, wide[:, 0], wide[:, 1]], axis=3).reshape(Z * C, 2 * strip_rows, 5 * rows)
    top = lax.all_to_all(top, ("z", "c"), 0, 0, tiled=True)
    top = top.reshape(Z * C, 2, strip_rows, 5 * rows).transpose(1, 0, 2, 3).reshape(width, 5 * rows)
    top, terms = lax.optimization_barrier((top, terms))
    top_own, top_rows = top[:, width:width + rows], top[:, width + rows:]
    update = jnp.sum(lax.all_to_all(terms, "z", 0, 0, tiled=True).astype(F32), axis=0)

    (inverse,) = in_vmem(inverse_factor, [(width, width)], (width, 2 * width), "inverse_factor", top[:, :width])
    level = jnp.dot(inverse, jnp.concatenate([top_own, top_rows], axis=1), precision=HI).astype(BF16)
    level_own = level[:, :rows]
    level_rows = level[:, rows:]

    schur = separator - update
    outer = lax.dot_general(
        level_rows, level_own, (((0,), (0,)), ((), ())), preferred_element_type=F32
    )
    keep = ((z > 0) | (c > 0)) & ((y > 0) | (x > 1))
    schur_next = jnp.where(keep, schur - outer, jnp.float32(0.0))
    return (panels, level_own, schur_next)


def solution(mesh):
    fine = Mesh(mesh.devices.reshape(Z, C, Y, X), ("z", "c", "y", "x"))
    grp, rd = ("z", "c"), ("y", "x")
    return jax.shard_map(
        body,
        mesh=fine,
        in_specs=(
            P(grp, rd, None),
            P(grp, None, None),
            P(grp, None),
            P(grp),
            P(grp, rd),
        ),
        out_specs=(P(grp, rd, None), P(None, rd), P(grp, rd)),
        check_vma=False,
    )
```

```python
import jax
import jax.numpy as jnp
from jax import lax
from jax.experimental import pallas as pl
from jax.experimental.pallas import tpu as pltpu
from jax.sharding import Mesh, PartitionSpec as P

Z, C, Y, X = 8, 2, 8, 4
GROUP = ("zh", "zl", "c")
HI = lax.Precision.HIGHEST
F32 = jnp.float32
BF16 = jnp.bfloat16
BLOCK, LANES, SUB = 64, 128, 8


def dot_t(a, b, out=F32):
    return lax.dot_general(a, b, (((1,), (1,)), ((), ())), preferred_element_type=out)


def share(array, axis, size):
    copies = jnp.broadcast_to(array[None], (size,) + array.shape)
    return lax.all_to_all(copies, axis, 0, 0, tiled=True)


def lane(tile, k):
    return jnp.broadcast_to(tile[:, k:k + 1], tile.shape)

def sub(tile, s):
    return jnp.broadcast_to(tile[s:s + 1, :], tile.shape)

def group_rows(tile, start):
    r = [sub(tile, s) for s in range(SUB)]
    d = [[lane(r[i], start + j) if j >= i else None for j in range(SUB)] for i in range(SUB)]
    pairs = []
    for p in range(0, SUB, 2):
        a, b, e = d[p][p], d[p][p + 1], d[p + 1][p + 1]
        inv = 1.0 / (a * e - b * b)
        ia, ib, ie = a * inv, b * inv, e * inv
        raw, low = {}, {}
        for i in range(p + 2, SUB):
            raw[i] = (e * d[p][i] - b * d[p + 1][i], a * d[p + 1][i] - b * d[p][i])
        for i in range(p + 2, SUB):
            for j in range(i, SUB):
                d[i][j] = d[i][j] - inv * (raw[i][0] * d[p][j] + raw[i][1] * d[p + 1][j])
            low[i] = (raw[i][0] * inv, raw[i][1] * inv)
            r[i] = r[i] - (low[i][0] * r[p] + low[i][1] * r[p + 1])
        pairs.append((a, b, e, ia, ib, ie, low))
    solved = [None] * SUB
    for p in range(SUB - 2, -1, -2):
        a, b, e, ia, ib, ie, low = pairs[p // 2]
        s0 = ie * r[p] - ib * r[p + 1]
        s1 = ia * r[p + 1] - ib * r[p]
        for i in range(p + 2, SUB):
            s0 = s0 - low[i][0] * solved[i]
            s1 = s1 - low[i][1] * solved[i]
        solved[p], solved[p + 1] = s0, s1
    norm = [None] * SUB
    for p in range(0, SUB, 2):
        a, b, e = pairs[p // 2][:3]
        ratio = b / a
        norm[p] = r[p] * lax.rsqrt(a)
        norm[p + 1] = (r[p + 1] - ratio * r[p]) * lax.rsqrt(e - ratio * b)
    return norm, solved

def block_inverse(block):
    n = BLOCK
    rowid = lax.broadcasted_iota(jnp.int32, (SUB, LANES), 0)
    laneid = lax.broadcasted_iota(jnp.int32, (SUB, LANES), 1)
    wide = jnp.concatenate([block, jnp.zeros((n, LANES - n), F32)], axis=1)
    tiles = []
    for t in range(n // SUB):
        unit = jnp.where(laneid == rowid + (n + t * SUB), 1.0, 0.0).astype(F32)
        tiles.append(wide[t * SUB:(t + 1) * SUB, :] + unit)
    for t in range(len(tiles)):
        norm, solved = group_rows(tiles[t], t * SUB)
        for u in range(t + 1, len(tiles)):
            terms = [lane(tiles[u], t * SUB + s) * solved[s] for s in range(SUB)]
            while len(terms) > 1:
                terms = [x + y for x, y in zip(terms[::2], terms[1::2])]
            tiles[u] = tiles[u] - terms[0]
        out = norm[0]
        for s in range(1, SUB):
            out = jnp.where(rowid == s, norm[s], out)
        tiles[t] = out
    return jnp.concatenate(tiles, axis=0)[:, n:]


def eliminate(aug, w_ref, s_row, start):
    n = aug.shape[1] // 2
    count = aug.shape[0]
    for k in range(0, w_ref.shape[0], BLOCK):
        rows = aug[k:k + BLOCK, :]
        inv = block_inverse(rows[:, start + k:start + k + BLOCK])
        u = jnp.dot(inv, rows, precision=HI, preferred_element_type=F32)
        w_ref[k:k + BLOCK, :] = u[:, n:] * s_row
        for m in range(k + BLOCK, count, BLOCK):
            left = u[:, start + m:start + m + BLOCK]
            aug[m:m + BLOCK, :] = aug[m:m + BLOCK, :] - lax.dot_general(
                left, u, (((0,), (0,)), ((), ())), precision=HI, preferred_element_type=F32
            )


def inverse_factor(a_ref, w_ref, aug):
    n = a_ref.shape[0]
    a = a_ref[:, :n]
    a = a * 0.5 + a.T * 0.5
    ri = lax.broadcasted_iota(jnp.int32, (n, n), 0)
    ci = lax.broadcasted_iota(jnp.int32, (n, n), 1)
    diag = jnp.where(ri == ci, a, 0.0)
    s_row = lax.rsqrt(jnp.sum(diag, axis=0, keepdims=True))
    s_col = lax.rsqrt(jnp.sum(diag, axis=1, keepdims=True))
    aug[:, :n] = a * s_col * s_row
    aug[:, n:] = jnp.where(ri == ci, 1.0, 0.0)
    eliminate(aug, w_ref, s_row, 0)


def in_vmem(body, outs, scratch, name, *args):
    spec = pl.BlockSpec(memory_space=pltpu.VMEM)
    return pl.pallas_call(
        body,
        out_shape=[jax.ShapeDtypeStruct(shape, F32) for shape in outs],
        in_specs=[spec] * len(args),
        out_specs=[spec] * len(outs),
        scratch_shapes=[pltpu.VMEM(scratch, F32)],
        compiler_params=pltpu.CompilerParams(vmem_limit_bytes=32 * 1024 * 1024),
        cost_estimate=pl.CostEstimate(flops=10**10, bytes_accessed=10**6, transcendentals=0),
        name=name,
    )(*args)


def leaf_panels(
    rows_hbm, inverse_hbm, pattern_hbm, widths_hbm, panels_ref, copies_ref,
    rows_ref, inverse_ref, pattern_ref, widths_ref, sems
):
    moves = [
        pltpu.make_async_copy(src, dst, sems.at[i])
        for i, (src, dst) in enumerate((
            (widths_hbm, widths_ref), (pattern_hbm, pattern_ref), (rows_hbm, rows_ref), (inverse_hbm, inverse_ref)
        ))
    ]
    for move in moves:
        move.start()
    for move in moves:
        move.wait()
    count, rows, width = rows_ref.shape
    at = 2 * lax.axis_index("y") + lax.div(lax.axis_index("x"), 2)
    lanes = lax.broadcasted_iota(jnp.int32, (rows, width), 1)
    for j in range(count):
        product = lax.dot_general(
            rows_ref[j], inverse_ref[j], (((1,), (1,)), ((), ())), precision=HI, preferred_element_type=F32
        )
        col_mask = (lanes < widths_ref[j]).astype(F32)
        panel = (product * pattern_ref[j, at].astype(F32) * col_mask).astype(BF16)
        panels_ref[j] = panel
        for k in range(copies_ref.shape[0]):
            copies_ref[k, :, j * width:(j + 1) * width] = panel


def body(leaf_rows, leaf_inverse, block_pattern, leaf_widths, separator):
    count, rows, width = leaf_rows.shape
    zh, zl, c, y, x = (lax.axis_index(a) for a in GROUP + ("y", "x"))
    z = 2 * zh + zl
    even = x % 2 == 0

    depth = count * width
    anywhere, vmem = pl.BlockSpec(memory_space=pl.ANY), pl.BlockSpec(memory_space=pltpu.VMEM)
    panels, copies = pl.pallas_call(
        leaf_panels,
        out_shape=[
            jax.ShapeDtypeStruct((count, rows, width), BF16),
            jax.ShapeDtypeStruct((Y, rows, depth), BF16),
        ],
        in_specs=[anywhere] * 4,
        out_specs=[vmem, vmem],
        scratch_shapes=[
            pltpu.VMEM(leaf_rows.shape, F32),
            pltpu.VMEM(leaf_inverse.shape, F32),
            pltpu.SMEM(block_pattern.shape, jnp.int32),
            pltpu.SMEM(leaf_widths.shape, jnp.int32),
            pltpu.SemaphoreType.DMA((4,)),
        ],
        compiler_params=pltpu.CompilerParams(vmem_limit_bytes=56 * 1024 * 1024),
        name="leaf_panels",
    )(leaf_rows, leaf_inverse, block_pattern, leaf_widths)
    own = copies[0]

    along_y = lax.all_to_all(copies, "y", 0, 0, tiled=True)
    shifted = [own] + [lax.ppermute(own, "x", [(i, (i + k) % X) for i in range(X)]) for k in range(1, X)]

    def choose(blocks, place):
        found = blocks[0]
        for k in range(1, X):
            found = jnp.where((x - place) % X == k, blocks[k], found)
        return found

    def gather_base(*moves):
        rows_of = separator[:rows], separator[rows:]
        to_lower = jnp.zeros((), bool)
        for src, dst in moves:
            to_lower |= (x == src) & (dst == 1)
        pairs = [(X * ys + src, X * ys + dst) for ys in range(Y) for src, dst in moves]
        return lax.ppermute(jnp.where(to_lower, rows_of[1], rows_of[0]), GROUP + ("y", "x"), pairs)

    swap, two, three = gather_base((0, 1), (1, 0)), gather_base((2, 0), (3, 1)), gather_base((3, 0), (2, 1))
    mine = jnp.where(even, separator[:rows], separator[rows:])
    base = [
        jnp.where(even, mine, swap),
        jnp.where(even, swap, mine),
        jnp.where(even, two, three),
        jnp.where(even, three, two),
    ]
    base = jnp.concatenate(base, axis=1)
    base = jnp.where((z == 0) & (c == 0) & (x < 2), base, jnp.zeros_like(base))
    block, base, *shifted = lax.optimization_barrier((along_y[0], base, *shifted))
    cols = [choose(shifted, place) for place in range(X)]

    strip_rows = rows // (Z * C)
    part = base - dot_t(block, jnp.concatenate(cols, axis=0))
    pieces = lax.all_to_all(part.reshape(Z * C, strip_rows, X * rows), GROUP, 0, 0, tiled=True)
    strip = jnp.sum(pieces, axis=0)
    strips = share(strip, ("y", "x"), Y * X).reshape(Y, X, strip_rows, X, rows)[:, :2]

    row_blocks = along_y.reshape(Y * rows, depth)
    theirs = jnp.concatenate([choose(shifted, 2 - 2 * c), choose(shifted, 3 - 2 * c)], axis=0)
    mine = jnp.concatenate([choose(shifted, 2 * c), choose(shifted, 2 * c + 1)], axis=0)
    sent = lax.ppermute(dot_t(row_blocks, theirs).astype(BF16), "c", [(0, 1), (1, 0)])
    terms = (dot_t(row_blocks, mine) + sent.astype(F32)).astype(BF16)
    blocks = terms.reshape(Z // 2, 2, rows, 2 * rows)
    give = jnp.where(zl == 0, blocks[:, 1], blocks[:, 0])
    got = lax.ppermute(give, "zl", [(0, 1), (1, 0)])
    strips, blocks, got = lax.optimization_barrier((strips, blocks, got))
    terms = jnp.where(zl == 0, blocks[:, 0], blocks[:, 1]).astype(F32) + got.astype(F32)
    terms = terms.astype(BF16).reshape(Z // 2 * rows, 2 * rows)

    def place(k):
        pairs = [(cs * X + xs, (xs // 2) * X + 2 * cs + ((xs % 2) ^ k)) for cs in range(C) for xs in range(X)]
        block = jnp.where((x % 2) ^ k == 0, terms[:, :rows], terms[:, rows:])
        return lax.ppermute(block, ("c", "x"), pairs).reshape(Z // 2, rows, rows)

    near, far = place(0), place(1)
    terms = jnp.concatenate([jnp.where(even, near, far), jnp.where(even, far, near)], axis=1)

    wide = strips.transpose(0, 3, 1, 2, 4)
    lead = jnp.concatenate([wide[0, 0], wide[0, 1], wide[y, x]], axis=2)
    lead = jnp.broadcast_to(lead[None], (Z * C,) + lead.shape)
    wide = wide.reshape(Z * C, 2, 2, strip_rows, rows)
    top = jnp.concatenate([lead, wide[:, 0], wide[:, 1]], axis=3).reshape(Z * C, 2 * strip_rows, 5 * rows)
    top = lax.all_to_all(top, GROUP, 0, 0, tiled=True)
    top = top.reshape(Z * C, 2, strip_rows, 5 * rows).transpose(1, 0, 2, 3).reshape(width, 5 * rows)
    top, terms = lax.optimization_barrier((top, terms))
    top_own, top_rows = top[:, width:width + rows], top[:, width + rows:]
    update = jnp.sum(lax.all_to_all(terms, "zh", 0, 0, tiled=True).astype(F32), axis=0)

    (inverse,) = in_vmem(inverse_factor, [(width, width)], (width, 2 * width), "inverse_factor", top[:, :width])
    inverse, update = lax.optimization_barrier((inverse, update))
    level = jnp.dot(inverse, jnp.concatenate([top_own, top_rows], axis=1), precision=HI).astype(BF16)
    level_own = level[:, :rows]
    level_rows = level[:, rows:]

    outer = lax.dot_general(
        level_rows, level_own, (((0,), (0,)), ((), ())), preferred_element_type=F32
    )
    keep = ((z > 0) | (c > 0)) & ((y > 0) | (x > 1))
    schur_next = jnp.where(keep, (separator - update) - outer, jnp.float32(0.0))
    return (panels, level_own, schur_next)


def solution(mesh):
    fine = Mesh(mesh.devices.reshape(Z // 2, 2, C, Y, X), GROUP + ("y", "x"))
    grp, rd = GROUP, ("y", "x")
    return jax.shard_map(
        body,
        mesh=fine,
        in_specs=(
            P(grp, rd, None),
            P(grp, None, None),
            P(grp, None),
            P(grp),
            P(grp, rd),
        ),
        out_specs=(P(grp, rd, None), P(None, rd), P(grp, rd)),
        check_vma=False,
    )
```

```python
import jax
import jax.numpy as jnp
from jax import lax
from jax.experimental import pallas as pl
from jax.experimental.pallas import tpu as pltpu
from jax.sharding import Mesh, PartitionSpec as P

Z, C, Y, X = 8, 2, 8, 4
GROUP = ("zh", "zl", "c")
HI = lax.Precision.HIGHEST
F32 = jnp.float32
BF16 = jnp.bfloat16
BLOCK, LANES, SUB = 64, 128, 8


def dot_t(a, b, out=F32):
    return lax.dot_general(a, b, (((1,), (1,)), ((), ())), preferred_element_type=out)


def share(array, axis, size):
    copies = jnp.broadcast_to(array[None], (size,) + array.shape)
    return lax.all_to_all(copies, axis, 0, 0, tiled=True)


def lane(tile, k):
    return jnp.broadcast_to(tile[:, k:k + 1], tile.shape)


def sub(tile, s):
    return jnp.broadcast_to(tile[s:s + 1, :], tile.shape)


def group_rows(tile, start, after):
    r = [sub(tile, s) for s in range(SUB)]
    d = [[lane(r[i], start + j) if j >= i else None for j in range(SUB)] for i in range(SUB)]
    c = [lane(after, start + j) for j in range(SUB)] if after is not None else None
    pairs = []
    for p in range(0, SUB, 2):
        a, b, e = d[p][p], d[p][p + 1], d[p + 1][p + 1]
        inv = 1.0 / (a * e - b * b)
        ia, ib, ie = a * inv, b * inv, e * inv
        raw, low = {}, {}
        for i in range(p + 2, SUB):
            raw[i] = (e * d[p][i] - b * d[p + 1][i], a * d[p + 1][i] - b * d[p][i])
        for i in range(p + 2, SUB):
            for j in range(i, SUB):
                d[i][j] = d[i][j] - inv * (raw[i][0] * d[p][j] + raw[i][1] * d[p + 1][j])
            low[i] = (raw[i][0] * inv, raw[i][1] * inv)
            r[i] = r[i] - (low[i][0] * r[p] + low[i][1] * r[p + 1])
        pairs.append((a, b, e, ia, ib, ie, low))
        if after is not None:
            after = after - (c[p] * (ie * r[p] - ib * r[p + 1]) + c[p + 1] * (ia * r[p + 1] - ib * r[p]))
            for i in range(p + 2, SUB):
                c[i] = c[i] - (low[i][0] * c[p] + low[i][1] * c[p + 1])
    solved = [None] * SUB
    for p in range(SUB - 2, -1, -2):
        a, b, e, ia, ib, ie, low = pairs[p // 2]
        s0 = ie * r[p] - ib * r[p + 1]
        s1 = ia * r[p + 1] - ib * r[p]
        for i in range(SUB - 1, p + 1, -1):
            s0 = s0 - low[i][0] * solved[i]
            s1 = s1 - low[i][1] * solved[i]
        solved[p], solved[p + 1] = s0, s1
    norm = [None] * SUB
    for p in range(0, SUB, 2):
        a, b, e = pairs[p // 2][:3]
        ratio = b / a
        norm[p] = r[p] * lax.rsqrt(a)
        norm[p + 1] = (r[p + 1] - ratio * r[p]) * lax.rsqrt(e - ratio * b)
    return norm, solved, after


def block_inverse(block):
    n = BLOCK
    rowid = lax.broadcasted_iota(jnp.int32, (SUB, LANES), 0)
    laneid = lax.broadcasted_iota(jnp.int32, (SUB, LANES), 1)
    wide = jnp.concatenate([block, jnp.zeros((n, LANES - n), F32)], axis=1)
    tiles = []
    for t in range(n // SUB):
        unit = jnp.where(laneid == rowid + (n + t * SUB), 1.0, 0.0).astype(F32)
        tiles.append(wide[t * SUB:(t + 1) * SUB, :] + unit)
    for t in range(len(tiles)):
        last = t + 1 == len(tiles)
        norm, solved, after = group_rows(tiles[t], t * SUB, None if last else tiles[t + 1])
        if not last:
            tiles[t + 1] = after
        for u in range(t + 2, len(tiles)):
            terms = [lane(tiles[u], t * SUB + s) * solved[s] for s in range(SUB)]
            while len(terms) > 1:
                terms = [x + y for x, y in zip(terms[::2], terms[1::2])]
            tiles[u] = tiles[u] - terms[0]
        out = norm[0]
        for s in range(1, SUB):
            out = jnp.where(rowid == s, norm[s], out)
        tiles[t] = out
    return jnp.concatenate(tiles, axis=0)[:, n:]


def inverse_factor(a_ref, w_ref, aug):
    n = a_ref.shape[0]
    a = a_ref[...]
    a = a * 0.5 + a.T * 0.5
    ri = lax.broadcasted_iota(jnp.int32, (n, n), 0)
    ci = lax.broadcasted_iota(jnp.int32, (n, n), 1)
    diag = jnp.where(ri == ci, a, 0.0)
    s_row = lax.rsqrt(jnp.sum(diag, axis=0, keepdims=True))
    s_col = lax.rsqrt(jnp.sum(diag, axis=1, keepdims=True))
    aug[:, :n] = a * s_col * s_row
    aug[:, n:] = jnp.where(ri == ci, 1.0, 0.0)
    for k in range(0, n, BLOCK):
        low, high = k // LANES * LANES, n + k + BLOCK
        rows = aug[k:k + BLOCK, low:high]
        inv = block_inverse(rows[:, k - low:k - low + BLOCK])
        u = jnp.dot(inv, rows, precision=HI, preferred_element_type=F32)
        w_ref[k:k + BLOCK, :] = jnp.zeros((BLOCK, n), F32)
        w_ref[k:k + BLOCK, :k + BLOCK] = u[:, n - low:] * s_row[:, :k + BLOCK]
        for m in range(k + BLOCK, n, BLOCK):
            left = u[:, m - low:m - low + BLOCK]
            aug[m:m + BLOCK, low:high] = aug[m:m + BLOCK, low:high] - lax.dot_general(
                left, u, (((0,), (0,)), ((), ())), precision=HI, preferred_element_type=F32
            )


def in_vmem(body, outs, scratch, name, *args):
    spec = pl.BlockSpec(memory_space=pltpu.VMEM)
    return pl.pallas_call(
        body,
        out_shape=[jax.ShapeDtypeStruct(shape, F32) for shape in outs],
        in_specs=[spec] * len(args),
        out_specs=[spec] * len(outs),
        scratch_shapes=[pltpu.VMEM(scratch, F32)],
        compiler_params=pltpu.CompilerParams(vmem_limit_bytes=32 * 1024 * 1024),
        cost_estimate=pl.CostEstimate(flops=10**10, bytes_accessed=10**6, transcendentals=0),
        name=name,
    )(*args)


def leaf_panels(
    rows_hbm, inverse_hbm, pattern_hbm, widths_hbm, panels_ref, copies_ref,
    rows_ref, inverse_ref, pattern_ref, widths_ref, sems
):
    moves = [
        pltpu.make_async_copy(src, dst, sems.at[i])
        for i, (src, dst) in enumerate((
            (widths_hbm, widths_ref), (pattern_hbm, pattern_ref), (rows_hbm, rows_ref), (inverse_hbm, inverse_ref)
        ))
    ]
    for move in moves:
        move.start()
    for move in moves:
        move.wait()
    count, rows, width = rows_ref.shape
    at = 2 * lax.axis_index("y") + lax.div(lax.axis_index("x"), 2)
    lanes = lax.broadcasted_iota(jnp.int32, (rows, width), 1)
    for j in range(count):
        product = lax.dot_general(
            rows_ref[j], inverse_ref[j], (((1,), (1,)), ((), ())), precision=HI, preferred_element_type=F32
        )
        col_mask = (lanes < widths_ref[j]).astype(F32)
        panel = (product * pattern_ref[j, at].astype(F32) * col_mask).astype(BF16)
        panels_ref[j] = panel
        for k in range(copies_ref.shape[0]):
            copies_ref[k, :, j * width:(j + 1) * width] = panel


def body(leaf_rows, leaf_inverse, block_pattern, leaf_widths, separator):
    count, rows, width = leaf_rows.shape
    zh, zl, c, y, x = (lax.axis_index(a) for a in GROUP + ("y", "x"))
    z = 2 * zh + zl
    even = x % 2 == 0

    depth = count * width
    anywhere, vmem = pl.BlockSpec(memory_space=pl.ANY), pl.BlockSpec(memory_space=pltpu.VMEM)
    panels, copies = pl.pallas_call(
        leaf_panels,
        out_shape=[
            jax.ShapeDtypeStruct((count, rows, width), BF16),
            jax.ShapeDtypeStruct((Y, rows, depth), BF16),
        ],
        in_specs=[anywhere] * 4,
        out_specs=[vmem, vmem],
        scratch_shapes=[
            pltpu.VMEM(leaf_rows.shape, F32),
            pltpu.VMEM(leaf_inverse.shape, F32),
            pltpu.SMEM(block_pattern.shape, jnp.int32),
            pltpu.SMEM(leaf_widths.shape, jnp.int32),
            pltpu.SemaphoreType.DMA((4,)),
        ],
        compiler_params=pltpu.CompilerParams(vmem_limit_bytes=56 * 1024 * 1024),
        name="leaf_panels",
    )(leaf_rows, leaf_inverse, block_pattern, leaf_widths)
    own = copies[0]

    along_y = lax.all_to_all(copies, "y", 0, 0, tiled=True)
    shifted = [own] + [lax.ppermute(own, "x", [(i, (i + k) % X) for i in range(X)]) for k in range(1, X)]

    def choose(blocks, place):
        found = blocks[0]
        for k in range(1, X):
            found = jnp.where((x - place) % X == k, blocks[k], found)
        return found

    def gather_base(*moves):
        rows_of = separator[:rows], separator[rows:]
        to_lower = jnp.zeros((), bool)
        for src, dst in moves:
            to_lower |= (x == src) & (dst == 1)
        pairs = [(X * ys + src, X * ys + dst) for ys in range(Y) for src, dst in moves]
        return lax.ppermute(jnp.where(to_lower, rows_of[1], rows_of[0]), GROUP + ("y", "x"), pairs)

    swap, two, three = gather_base((0, 1), (1, 0)), gather_base((2, 0), (3, 1)), gather_base((3, 0), (2, 1))
    mine = jnp.where(even, separator[:rows], separator[rows:])
    base = [
        jnp.where(even, mine, swap),
        jnp.where(even, swap, mine),
        jnp.where(even, two, three),
        jnp.where(even, three, two),
    ]
    base = jnp.concatenate(base, axis=1)
    base = jnp.where((z == 0) & (c == 0) & (x < 2), base, jnp.zeros_like(base))
    block, base, *shifted = lax.optimization_barrier((along_y[0], base, *shifted))
    cols = [choose(shifted, place) for place in range(X)]

    strip_rows = rows // (Z * C)
    part = base - dot_t(block, jnp.concatenate(cols, axis=0))
    pieces = lax.all_to_all(part.reshape(Z * C, strip_rows, X * rows), GROUP, 0, 0, tiled=True)
    strip = jnp.sum(pieces, axis=0)
    strips = share(strip, ("y", "x"), Y * X).reshape(Y, X, strip_rows, X, rows)[:, :2]

    row_blocks = along_y.reshape(Y * rows, depth)
    theirs = jnp.concatenate([choose(shifted, 2 - 2 * c), choose(shifted, 3 - 2 * c)], axis=0)
    mine = jnp.concatenate([choose(shifted, 2 * c), choose(shifted, 2 * c + 1)], axis=0)
    sent = lax.ppermute(dot_t(row_blocks, theirs).astype(BF16), "c", [(0, 1), (1, 0)])
    terms = (dot_t(row_blocks, mine) + sent.astype(F32)).astype(BF16)
    blocks = terms.reshape(Z // 2, 2, rows, 2 * rows)
    give = jnp.where(zl == 0, blocks[:, 1], blocks[:, 0])
    got = lax.ppermute(give, "zl", [(0, 1), (1, 0)])
    strips, blocks, got = lax.optimization_barrier((strips, blocks, got))
    terms = jnp.where(zl == 0, blocks[:, 0], blocks[:, 1]).astype(F32) + got.astype(F32)
    terms = terms.astype(BF16).reshape(Z // 2 * rows, 2 * rows)

    def place(k):
        pairs = [(cs * X + xs, (xs // 2) * X + 2 * cs + ((xs % 2) ^ k)) for cs in range(C) for xs in range(X)]
        block = jnp.where((x % 2) ^ k == 0, terms[:, :rows], terms[:, rows:])
        return lax.ppermute(block, ("c", "x"), pairs).reshape(Z // 2, rows, rows)

    near, far = place(0), place(1)
    terms = jnp.concatenate([jnp.where(even, near, far), jnp.where(even, far, near)], axis=1)

    wide = strips.transpose(0, 3, 1, 2, 4)
    lead = jnp.concatenate([wide[0, 0], wide[0, 1], wide[y, x]], axis=2)
    lead = jnp.broadcast_to(lead[None], (Z * C,) + lead.shape)
    wide = wide.reshape(Z * C, 2, 2, strip_rows, rows)
    top = jnp.concatenate([lead, wide[:, 0], wide[:, 1]], axis=3).reshape(Z * C, 2 * strip_rows, 5 * rows)
    top = lax.all_to_all(top, GROUP, 0, 0, tiled=True)
    top = top.reshape(Z * C, 2, strip_rows, 5 * rows).transpose(1, 0, 2, 3).reshape(width, 5 * rows)
    top, terms = lax.optimization_barrier((top, terms))
    top_own, top_rows = top[:, width:width + rows], top[:, width + rows:]
    update = jnp.sum(lax.all_to_all(terms, "zh", 0, 0, tiled=True).astype(F32), axis=0)

    (inverse,) = in_vmem(inverse_factor, [(width, width)], (width, 2 * width), "inverse_factor", top[:, :width])
    inverse, update = lax.optimization_barrier((inverse, update))
    level = jnp.dot(inverse, jnp.concatenate([top_own, top_rows], axis=1), precision=HI).astype(BF16)
    level_own = level[:, :rows]
    level_rows = level[:, rows:]

    outer = lax.dot_general(
        level_rows, level_own, (((0,), (0,)), ((), ())), preferred_element_type=F32
    )
    keep = ((z > 0) | (c > 0)) & ((y > 0) | (x > 1))
    schur_next = jnp.where(keep, (separator - update) - outer, jnp.float32(0.0))
    return (panels, level_own, schur_next)


def solution(mesh):
    fine = Mesh(mesh.devices.reshape(Z // 2, 2, C, Y, X), GROUP + ("y", "x"))
    grp, rd = GROUP, ("y", "x")
    return jax.shard_map(
        body,
        mesh=fine,
        in_specs=(
            P(grp, rd, None),
            P(grp, None, None),
            P(grp, None),
            P(grp),
            P(grp, rd),
        ),
        out_specs=(P(grp, rd, None), P(None, rd), P(grp, rd)),
        check_vma=False,
    )
```

```python
import jax
import jax.numpy as jnp
from jax import lax
from jax.experimental import pallas as pl
from jax.experimental.pallas import tpu as pltpu
from jax.sharding import Mesh, PartitionSpec as P

Z, C, Y, X = 8, 2, 8, 4
GROUP = ("zh", "zl", "c")
HI = lax.Precision.HIGHEST
F32 = jnp.float32
BF16 = jnp.bfloat16
BLOCK, LANES, SUB = 64, 128, 8


def dot_t(a, b, out=F32):
    return lax.dot_general(a, b, (((1,), (1,)), ((), ())), preferred_element_type=out)


def share(array, axis, size):
    copies = jnp.broadcast_to(array[None], (size,) + array.shape)
    return lax.all_to_all(copies, axis, 0, 0, tiled=True)


def lane(tile, k):
    return jnp.broadcast_to(tile[:, k:k + 1], tile.shape)


def sub(tile, s):
    return jnp.broadcast_to(tile[s:s + 1, :], tile.shape)


def group_rows(tile, start, after):
    r = [sub(tile, s) for s in range(SUB)]
    d = [[lane(r[i], start + j) if j >= i else None for j in range(SUB)] for i in range(SUB)]
    c = [lane(after, start + j) for j in range(SUB)] if after is not None else None
    pairs = []
    for p in range(0, SUB, 2):
        a, b, e = d[p][p], d[p][p + 1], d[p + 1][p + 1]
        inv = 1.0 / (a * e - b * b)
        ia, ib, ie = a * inv, b * inv, e * inv
        raw, low = {}, {}
        for i in range(p + 2, SUB):
            raw[i] = (e * d[p][i] - b * d[p + 1][i], a * d[p + 1][i] - b * d[p][i])
        for i in range(p + 2, SUB):
            for j in range(i, SUB):
                d[i][j] = d[i][j] - inv * (raw[i][0] * d[p][j] + raw[i][1] * d[p + 1][j])
            low[i] = (raw[i][0] * inv, raw[i][1] * inv)
            r[i] = r[i] - (low[i][0] * r[p] + low[i][1] * r[p + 1])
        pairs.append((a, b, e, ia, ib, ie, low))
        if after is not None:
            after = after - (c[p] * (ie * r[p] - ib * r[p + 1]) + c[p + 1] * (ia * r[p + 1] - ib * r[p]))
            for i in range(p + 2, SUB):
                c[i] = c[i] - (low[i][0] * c[p] + low[i][1] * c[p + 1])
    solved = [None] * SUB
    for p in range(SUB - 2, -1, -2):
        a, b, e, ia, ib, ie, low = pairs[p // 2]
        s0 = ie * r[p] - ib * r[p + 1]
        s1 = ia * r[p + 1] - ib * r[p]
        for i in range(SUB - 1, p + 1, -1):
            s0 = s0 - low[i][0] * solved[i]
            s1 = s1 - low[i][1] * solved[i]
        solved[p], solved[p + 1] = s0, s1
    norm = [None] * SUB
    for p in range(0, SUB, 2):
        a, b, e = pairs[p // 2][:3]
        ratio = b / a
        norm[p] = r[p] * lax.rsqrt(a)
        norm[p + 1] = (r[p + 1] - ratio * r[p]) * lax.rsqrt(e - ratio * b)
    return norm, solved, after


def block_inverse(block):
    n = BLOCK
    rowid = lax.broadcasted_iota(jnp.int32, (SUB, LANES), 0)
    laneid = lax.broadcasted_iota(jnp.int32, (SUB, LANES), 1)
    wide = jnp.concatenate([block, jnp.zeros((n, LANES - n), F32)], axis=1)
    tiles = []
    for t in range(n // SUB):
        unit = jnp.where(laneid == rowid + (n + t * SUB), 1.0, 0.0).astype(F32)
        tiles.append(wide[t * SUB:(t + 1) * SUB, :] + unit)
    for t in range(len(tiles)):
        last = t + 1 == len(tiles)
        norm, solved, after = group_rows(tiles[t], t * SUB, None if last else tiles[t + 1])
        if not last:
            tiles[t + 1] = after
        for u in range(t + 2, len(tiles)):
            terms = [lane(tiles[u], t * SUB + s) * solved[s] for s in range(SUB)]
            while len(terms) > 1:
                terms = [x + y for x, y in zip(terms[::2], terms[1::2])]
            tiles[u] = tiles[u] - terms[0]
        out = norm[0]
        for s in range(1, SUB):
            out = jnp.where(rowid == s, norm[s], out)
        tiles[t] = out
    return jnp.concatenate(tiles, axis=0)[:, n:]


def inverse_factor(upper_ref, lower_ref, w_ref, aug):
    n = lower_ref.shape[1]
    corner = lower_ref[:, :n // 2].T
    a = jnp.concatenate([jnp.concatenate([upper_ref[...], corner], axis=1), lower_ref[...]], axis=0)
    a = a * 0.5 + a.T * 0.5
    ri = lax.broadcasted_iota(jnp.int32, (n, n), 0)
    ci = lax.broadcasted_iota(jnp.int32, (n, n), 1)
    diag = jnp.where(ri == ci, a, 0.0)
    s_row = lax.rsqrt(jnp.sum(diag, axis=0, keepdims=True))
    s_col = lax.rsqrt(jnp.sum(diag, axis=1, keepdims=True))
    aug[:, :n] = a * s_col * s_row
    aug[:, n:] = jnp.where(ri == ci, 1.0, 0.0)
    for k in range(0, n, BLOCK):
        low, high = k // LANES * LANES, n + k + BLOCK
        rows = aug[k:k + BLOCK, low:high]
        inv = block_inverse(rows[:, k - low:k - low + BLOCK])
        u = jnp.dot(inv, rows, precision=HI, preferred_element_type=F32)
        w_ref[k:k + BLOCK, :] = jnp.zeros((BLOCK, n), F32)
        w_ref[k:k + BLOCK, :k + BLOCK] = u[:, n - low:] * s_row[:, :k + BLOCK]
        for m in range(k + BLOCK, n, BLOCK):
            left = u[:, m - low:m - low + BLOCK]
            aug[m:m + BLOCK, low:high] = aug[m:m + BLOCK, low:high] - lax.dot_general(
                left, u, (((0,), (0,)), ((), ())), precision=HI, preferred_element_type=F32
            )


def in_vmem(body, outs, scratch, name, *args):
    spec = pl.BlockSpec(memory_space=pltpu.VMEM)
    return pl.pallas_call(
        body,
        out_shape=[jax.ShapeDtypeStruct(shape, F32) for shape in outs],
        in_specs=[spec] * len(args),
        out_specs=[spec] * len(outs),
        scratch_shapes=[pltpu.VMEM(scratch, F32)],
        compiler_params=pltpu.CompilerParams(vmem_limit_bytes=32 * 1024 * 1024),
        cost_estimate=pl.CostEstimate(flops=10**10, bytes_accessed=10**6, transcendentals=0),
        name=name,
    )(*args)


def first_rows(strips_ref, top_ref, unused):
    y, x = lax.axis_index("y"), lax.axis_index("x")
    lane_at = pl.ds(pl.multiple_of(x * LANES, LANES), LANES)

    def cut(line, row, at):
        return strips_ref[X * line + row, :, at * LANES:(at + 1) * LANES]

    common = []
    for row in range(2):
        lead = [cut(0, row, at) for at in range(row + 1)]
        common.append(lead + [strips_ref[X * y + row, :, lane_at]])
    for g in range(top_ref.shape[0]):
        parts = []
        for row in range(2):
            parts += common[row] + [cut(g // 2, row, 2 * (g % 2) + b) for b in range(2)]
        for i, part in enumerate(parts):
            top_ref[g, :, i * LANES:(i + 1) * LANES] = part


def leaf_panels(
    rows_hbm, inverse_hbm, pattern_hbm, widths_hbm, panels_ref, copies_ref,
    rows_ref, inverse_ref, pattern_ref, widths_ref, sems
):
    moves = [
        pltpu.make_async_copy(src, dst, sems.at[i])
        for i, (src, dst) in enumerate((
            (widths_hbm, widths_ref), (pattern_hbm, pattern_ref), (rows_hbm, rows_ref), (inverse_hbm, inverse_ref)
        ))
    ]
    for move in moves:
        move.start()
    for move in moves:
        move.wait()
    count, rows, width = rows_ref.shape
    at = 2 * lax.axis_index("y") + lax.div(lax.axis_index("x"), 2)
    lanes = lax.broadcasted_iota(jnp.int32, (rows, width), 1)
    for j in range(count):
        product = lax.dot_general(
            rows_ref[j], inverse_ref[j], (((1,), (1,)), ((), ())), precision=HI, preferred_element_type=F32
        )
        col_mask = (lanes < widths_ref[j]).astype(F32)
        panel = (product * pattern_ref[j, at].astype(F32) * col_mask).astype(BF16)
        panels_ref[j] = panel
        for k in range(copies_ref.shape[0]):
            copies_ref[k, :, j * width:(j + 1) * width] = panel


def body(leaf_rows, leaf_inverse, block_pattern, leaf_widths, separator):
    count, rows, width = leaf_rows.shape
    zh, zl, c, y, x = (lax.axis_index(a) for a in GROUP + ("y", "x"))
    z = 2 * zh + zl
    even = x % 2 == 0

    depth = count * width
    anywhere, vmem = pl.BlockSpec(memory_space=pl.ANY), pl.BlockSpec(memory_space=pltpu.VMEM)
    panels, copies = pl.pallas_call(
        leaf_panels,
        out_shape=[
            jax.ShapeDtypeStruct((count, rows, width), BF16),
            jax.ShapeDtypeStruct((Y, rows, depth), BF16),
        ],
        in_specs=[anywhere] * 4,
        out_specs=[vmem, vmem],
        scratch_shapes=[
            pltpu.VMEM(leaf_rows.shape, F32),
            pltpu.VMEM(leaf_inverse.shape, F32),
            pltpu.SMEM(block_pattern.shape, jnp.int32),
            pltpu.SMEM(leaf_widths.shape, jnp.int32),
            pltpu.SemaphoreType.DMA((4,)),
        ],
        compiler_params=pltpu.CompilerParams(vmem_limit_bytes=56 * 1024 * 1024),
        name="leaf_panels",
    )(leaf_rows, leaf_inverse, block_pattern, leaf_widths)
    own = copies[0]

    along_y = lax.all_to_all(copies, "y", 0, 0, tiled=True)
    shifted = [own] + [lax.ppermute(own, "x", [(i, (i + k) % X) for i in range(X)]) for k in range(1, X)]

    def choose(blocks, place):
        found = blocks[0]
        for k in range(1, X):
            found = jnp.where((x - place) % X == k, blocks[k], found)
        return found

    def gather_base(*moves):
        rows_of = separator[:rows], separator[rows:]
        to_lower = jnp.zeros((), bool)
        for src, dst in moves:
            to_lower |= (x == src) & (dst == 1)
        pairs = [(X * ys + src, X * ys + dst) for ys in range(Y) for src, dst in moves]
        return lax.ppermute(jnp.where(to_lower, rows_of[1], rows_of[0]), GROUP + ("y", "x"), pairs)

    swap, two, three = gather_base((0, 1), (1, 0)), gather_base((2, 0), (3, 1)), gather_base((3, 0), (2, 1))
    mine = jnp.where(even, separator[:rows], separator[rows:])
    base = [
        jnp.where(even, mine, swap),
        jnp.where(even, swap, mine),
        jnp.where(even, two, three),
        jnp.where(even, three, two),
    ]
    base = jnp.concatenate(base, axis=1)
    base = jnp.where((z == 0) & (c == 0) & (x < 2), base, jnp.zeros_like(base))
    block, base, *shifted = lax.optimization_barrier((along_y[0], base, *shifted))
    cols = [choose(shifted, place) for place in range(X)]

    strip_rows = rows // (Z * C)
    part = base - dot_t(block, jnp.concatenate(cols, axis=0))
    pieces = lax.all_to_all(part.reshape(Z * C, strip_rows, X * rows), GROUP, 0, 0, tiled=True)
    strip = jnp.sum(pieces, axis=0)
    strips = share(strip, ("y", "x"), Y * X)

    row_blocks = along_y.reshape(Y * rows, depth)
    theirs = jnp.concatenate([choose(shifted, 2 - 2 * c), choose(shifted, 3 - 2 * c)], axis=0)
    mine = jnp.concatenate([choose(shifted, 2 * c), choose(shifted, 2 * c + 1)], axis=0)
    sent = lax.ppermute(dot_t(row_blocks, theirs).astype(BF16), "c", [(0, 1), (1, 0)])
    terms = (dot_t(row_blocks, mine) + sent.astype(F32)).astype(BF16)
    blocks = terms.reshape(Z // 2, 2, rows, 2 * rows)
    give = jnp.where(zl == 0, blocks[:, 1], blocks[:, 0])
    got = lax.ppermute(give, "zl", [(0, 1), (1, 0)])
    strips, blocks, got = lax.optimization_barrier((strips, blocks, got))
    terms = jnp.where(zl == 0, blocks[:, 0], blocks[:, 1]).astype(F32) + got.astype(F32)
    terms = terms.astype(BF16).reshape(Z // 2 * rows, 2 * rows)

    def place(k):
        pairs = [(cs * X + xs, (xs // 2) * X + 2 * cs + ((xs % 2) ^ k)) for cs in range(C) for xs in range(X)]
        block = jnp.where((x % 2) ^ k == 0, terms[:, :rows], terms[:, rows:])
        return lax.ppermute(block, ("c", "x"), pairs).reshape(Z // 2, rows, rows)

    near, far = place(0), place(1)
    terms = jnp.concatenate([jnp.where(even, near, far), jnp.where(even, far, near)], axis=1)

    (top,) = in_vmem(first_rows, [(Z * C, strip_rows, 9 * rows)], (SUB, LANES), "first_rows", strips)
    top = lax.all_to_all(top, GROUP, 0, 0, tiled=True).reshape(rows, 9 * rows)
    top, terms = lax.optimization_barrier((top, terms))
    top_cols = jnp.concatenate([top[:, rows:4 * rows], top[:, 6 * rows:]], axis=0)
    update = jnp.sum(lax.all_to_all(terms, "zh", 0, 0, tiled=True).astype(F32), axis=0)

    (inverse,) = in_vmem(inverse_factor, [(width, width)], (width, 2 * width), "inverse_factor", top[:, :rows], top[:, 4 * rows:6 * rows])
    inverse, update = lax.optimization_barrier((inverse, update))
    level = jnp.dot(inverse, top_cols, precision=HI).astype(BF16)
    level_own = level[:, :rows]
    level_rows = level[:, rows:]

    outer = lax.dot_general(
        level_rows, level_own, (((0,), (0,)), ((), ())), preferred_element_type=F32
    )
    keep = ((z > 0) | (c > 0)) & ((y > 0) | (x > 1))
    schur_next = jnp.where(keep, (separator - update) - outer, jnp.float32(0.0))
    return (panels, level_own, schur_next)


def solution(mesh):
    fine = Mesh(mesh.devices.reshape(Z // 2, 2, C, Y, X), GROUP + ("y", "x"))
    grp, rd = GROUP, ("y", "x")
    return jax.shard_map(
        body,
        mesh=fine,
        in_specs=(
            P(grp, rd, None),
            P(grp, None, None),
            P(grp, None),
            P(grp),
            P(grp, rd),
        ),
        out_specs=(P(grp, rd, None), P(None, rd), P(grp, rd)),
        check_vma=False,
    )
```

```python
import jax
import jax.numpy as jnp
from jax import lax
from jax.experimental import pallas as pl
from jax.experimental.pallas import tpu as pltpu
from jax.sharding import Mesh, PartitionSpec as P

Z, C, Y, X = 8, 2, 8, 4
GROUP = ("zh", "zl", "c")
HI = lax.Precision.HIGHEST
F32 = jnp.float32
BF16 = jnp.bfloat16
BLOCK, LANES, SUB = 64, 128, 8


def dot_t(a, b, out=F32):
    return lax.dot_general(a, b, (((1,), (1,)), ((), ())), preferred_element_type=out)


def lane(tile, k):
    return jnp.broadcast_to(tile[:, k:k + 1], tile.shape)


def sub(tile, s):
    return jnp.broadcast_to(tile[s:s + 1, :], tile.shape)


def group_rows(tile, start, after):
    r = [sub(tile, s) for s in range(SUB)]
    d = [[lane(r[i], start + j) if j >= i else None for j in range(SUB)] for i in range(SUB)]
    c = [lane(after, start + j) for j in range(SUB)] if after is not None else None
    pairs = []
    for p in range(0, SUB, 2):
        a, b, e = d[p][p], d[p][p + 1], d[p + 1][p + 1]
        inv = 1.0 / (a * e - b * b)
        ia, ib, ie = a * inv, b * inv, e * inv
        raw, low = {}, {}
        for i in range(p + 2, SUB):
            raw[i] = (e * d[p][i] - b * d[p + 1][i], a * d[p + 1][i] - b * d[p][i])
        for i in range(p + 2, SUB):
            for j in range(i, SUB):
                d[i][j] = d[i][j] - inv * (raw[i][0] * d[p][j] + raw[i][1] * d[p + 1][j])
            low[i] = (raw[i][0] * inv, raw[i][1] * inv)
            r[i] = r[i] - (low[i][0] * r[p] + low[i][1] * r[p + 1])
        pairs.append((a, b, e, ia, ib, ie, low))
        if after is not None:
            after = after - (c[p] * (ie * r[p] - ib * r[p + 1]) + c[p + 1] * (ia * r[p + 1] - ib * r[p]))
            for i in range(p + 2, SUB):
                c[i] = c[i] - (low[i][0] * c[p] + low[i][1] * c[p + 1])
    solved = [None] * SUB
    for p in range(SUB - 2, -1, -2):
        a, b, e, ia, ib, ie, low = pairs[p // 2]
        s0 = ie * r[p] - ib * r[p + 1]
        s1 = ia * r[p + 1] - ib * r[p]
        for i in range(SUB - 1, p + 1, -1):
            s0 = s0 - low[i][0] * solved[i]
            s1 = s1 - low[i][1] * solved[i]
        solved[p], solved[p + 1] = s0, s1
    norm = [None] * SUB
    for p in range(0, SUB, 2):
        a, b, e = pairs[p // 2][:3]
        ratio = b / a
        norm[p] = r[p] * lax.rsqrt(a)
        norm[p + 1] = (r[p + 1] - ratio * r[p]) * lax.rsqrt(e - ratio * b)
    return norm, solved, after


def block_inverse(block):
    n = BLOCK
    rowid = lax.broadcasted_iota(jnp.int32, (SUB, LANES), 0)
    laneid = lax.broadcasted_iota(jnp.int32, (SUB, LANES), 1)
    wide = jnp.concatenate([block, jnp.zeros((n, LANES - n), F32)], axis=1)
    tiles = []
    for t in range(n // SUB):
        unit = jnp.where(laneid == rowid + (n + t * SUB), 1.0, 0.0).astype(F32)
        tiles.append(wide[t * SUB:(t + 1) * SUB, :] + unit)
    for t in range(len(tiles)):
        last = t + 1 == len(tiles)
        norm, solved, after = group_rows(tiles[t], t * SUB, None if last else tiles[t + 1])
        if not last:
            tiles[t + 1] = after
        for u in range(t + 2, len(tiles)):
            terms = [lane(tiles[u], t * SUB + s) * solved[s] for s in range(SUB)]
            while len(terms) > 1:
                terms = [x + y for x, y in zip(terms[::2], terms[1::2])]
            tiles[u] = tiles[u] - terms[0]
        out = norm[0]
        for s in range(1, SUB):
            out = jnp.where(rowid == s, norm[s], out)
        tiles[t] = out
    return jnp.concatenate(tiles, axis=0)[:, n:]


def inverse_factor(upper_ref, lower_ref, w_ref, aug):
    n = lower_ref.shape[1]
    corner = lower_ref[:, :n // 2].T
    a = jnp.concatenate([jnp.concatenate([upper_ref[...], corner], axis=1), lower_ref[...]], axis=0)
    a = a * 0.5 + a.T * 0.5
    ri = lax.broadcasted_iota(jnp.int32, (n, n), 0)
    ci = lax.broadcasted_iota(jnp.int32, (n, n), 1)
    diag = jnp.where(ri == ci, a, 0.0)
    s_row = lax.rsqrt(jnp.sum(diag, axis=0, keepdims=True))
    s_col = lax.rsqrt(jnp.sum(diag, axis=1, keepdims=True))
    aug[:, :n] = a * s_col * s_row
    aug[:, n:] = jnp.where(ri == ci, 1.0, 0.0)
    for k in range(0, n, BLOCK):
        low, high = k // LANES * LANES, n + k + BLOCK
        rows = aug[k:k + BLOCK, low:high]
        inv = block_inverse(rows[:, k - low:k - low + BLOCK])
        u = jnp.dot(inv, rows, precision=HI, preferred_element_type=F32)
        w_ref[k:k + BLOCK, :] = jnp.zeros((BLOCK, n), F32)
        w_ref[k:k + BLOCK, :k + BLOCK] = u[:, n - low:] * s_row[:, :k + BLOCK]
        for m in range(k + BLOCK, n, BLOCK):
            left = u[:, m - low:m - low + BLOCK]
            aug[m:m + BLOCK, low:high] = aug[m:m + BLOCK, low:high] - lax.dot_general(
                left, u, (((0,), (0,)), ((), ())), precision=HI, preferred_element_type=F32
            )


def in_vmem(body, outs, scratch, name, *args):
    spec = pl.BlockSpec(memory_space=pltpu.VMEM)
    return pl.pallas_call(
        body,
        out_shape=[jax.ShapeDtypeStruct(shape, F32) for shape in outs],
        in_specs=[spec] * len(args),
        out_specs=[spec] * len(outs),
        scratch_shapes=[pltpu.VMEM(scratch, F32)],
        compiler_params=pltpu.CompilerParams(vmem_limit_bytes=32 * 1024 * 1024),
        cost_estimate=pl.CostEstimate(flops=10**10, bytes_accessed=10**6, transcendentals=0),
        name=name,
    )(*args)


def strip_copies(pieces_ref, copies_ref, unused):
    strip = pieces_ref[0]
    for g in range(1, pieces_ref.shape[0]):
        strip = strip + pieces_ref[g]
    for k in range(copies_ref.shape[0]):
        copies_ref[k] = strip


def first_rows(strips_ref, top_ref, unused):
    y, x = lax.axis_index("y"), lax.axis_index("x")
    lane_at = pl.ds(pl.multiple_of(x * LANES, LANES), LANES)

    def cut(line, row, at):
        return strips_ref[X * line + row, :, at * LANES:(at + 1) * LANES]

    common = []
    for row in range(2):
        lead = [cut(0, row, at) for at in range(row + 1)]
        common.append(lead + [strips_ref[X * y + row, :, lane_at]])
    for g in range(top_ref.shape[0]):
        parts = []
        for row in range(2):
            parts += common[row] + [cut(g // 2, row, 2 * (g % 2) + b) for b in range(2)]
        for i, part in enumerate(parts):
            top_ref[g, :, i * LANES:(i + 1) * LANES] = part


def leaf_panels(
    rows_hbm, inverse_hbm, pattern_hbm, widths_hbm, panels_ref, copies_ref,
    rows_ref, inverse_ref, pattern_ref, widths_ref, sems
):
    moves = [
        pltpu.make_async_copy(src, dst, sems.at[i])
        for i, (src, dst) in enumerate((
            (widths_hbm, widths_ref), (pattern_hbm, pattern_ref), (rows_hbm, rows_ref), (inverse_hbm, inverse_ref)
        ))
    ]
    for move in moves:
        move.start()
    for move in moves:
        move.wait()
    count, rows, width = rows_ref.shape
    at = 2 * lax.axis_index("y") + lax.div(lax.axis_index("x"), 2)
    lanes = lax.broadcasted_iota(jnp.int32, (rows, width), 1)
    for j in range(count):
        product = lax.dot_general(
            rows_ref[j], inverse_ref[j], (((1,), (1,)), ((), ())), precision=HI, preferred_element_type=F32
        )
        col_mask = (lanes < widths_ref[j]).astype(F32)
        panel = (product * pattern_ref[j, at].astype(F32) * col_mask).astype(BF16)
        panels_ref[j] = panel
        for k in range(copies_ref.shape[0]):
            copies_ref[k, :, j * width:(j + 1) * width] = panel


def body(leaf_rows, leaf_inverse, block_pattern, leaf_widths, separator):
    count, rows, width = leaf_rows.shape
    zh, zl, c, y, x = (lax.axis_index(a) for a in GROUP + ("y", "x"))
    z = 2 * zh + zl
    even = x % 2 == 0

    depth = count * width
    anywhere, vmem = pl.BlockSpec(memory_space=pl.ANY), pl.BlockSpec(memory_space=pltpu.VMEM)
    panels, copies = pl.pallas_call(
        leaf_panels,
        out_shape=[
            jax.ShapeDtypeStruct((count, rows, width), BF16),
            jax.ShapeDtypeStruct((Y, rows, depth), BF16),
        ],
        in_specs=[anywhere] * 4,
        out_specs=[vmem, vmem],
        scratch_shapes=[
            pltpu.VMEM(leaf_rows.shape, F32),
            pltpu.VMEM(leaf_inverse.shape, F32),
            pltpu.SMEM(block_pattern.shape, jnp.int32),
            pltpu.SMEM(leaf_widths.shape, jnp.int32),
            pltpu.SemaphoreType.DMA((4,)),
        ],
        compiler_params=pltpu.CompilerParams(vmem_limit_bytes=56 * 1024 * 1024),
        name="leaf_panels",
    )(leaf_rows, leaf_inverse, block_pattern, leaf_widths)
    own = copies[0]

    along_y = lax.all_to_all(copies, "y", 0, 0, tiled=True)
    shifted = [own] + [lax.ppermute(own, "x", [(i, (i + k) % X) for i in range(X)]) for k in range(1, X)]

    def choose(blocks, place):
        found = blocks[0]
        for k in range(1, X):
            found = jnp.where((x - place) % X == k, blocks[k], found)
        return found

    def gather_base(*moves):
        rows_of = separator[:rows], separator[rows:]
        to_lower = jnp.zeros((), bool)
        for src, dst in moves:
            to_lower |= (x == src) & (dst == 1)
        pairs = [(X * ys + src, X * ys + dst) for ys in range(Y) for src, dst in moves]
        return lax.ppermute(jnp.where(to_lower, rows_of[1], rows_of[0]), GROUP + ("y", "x"), pairs)

    swap, two, three = gather_base((0, 1), (1, 0)), gather_base((2, 0), (3, 1)), gather_base((3, 0), (2, 1))
    mine = jnp.where(even, separator[:rows], separator[rows:])
    base = [
        jnp.where(even, mine, swap),
        jnp.where(even, swap, mine),
        jnp.where(even, two, three),
        jnp.where(even, three, two),
    ]
    base = jnp.concatenate(base, axis=1)
    base = jnp.where((z == 0) & (c == 0) & (x < 2), base, jnp.zeros_like(base))
    block, base, *shifted = lax.optimization_barrier((along_y[0], base, *shifted))
    cols = [choose(shifted, place) for place in range(X)]

    strip_rows = rows // (Z * C)
    part = base - dot_t(block, jnp.concatenate(cols, axis=0))
    pieces = lax.all_to_all(part.reshape(Z * C, strip_rows, X * rows), GROUP, 0, 0, tiled=True)
    (strips,) = in_vmem(strip_copies, [(Y * X, strip_rows, X * rows)], (SUB, LANES), "strip_copies", pieces)
    strips = lax.all_to_all(strips, ("y", "x"), 0, 0, tiled=True)

    row_blocks = along_y.reshape(Y * rows, depth)
    theirs = jnp.concatenate([choose(shifted, 2 - 2 * c), choose(shifted, 3 - 2 * c)], axis=0)
    mine = jnp.concatenate([choose(shifted, 2 * c), choose(shifted, 2 * c + 1)], axis=0)
    sent = lax.ppermute(dot_t(row_blocks, theirs).astype(BF16), "c", [(0, 1), (1, 0)])
    terms = (dot_t(row_blocks, mine) + sent.astype(F32)).astype(BF16)
    blocks = terms.reshape(Z // 2, 2, rows, 2 * rows)
    give = jnp.where(zl == 0, blocks[:, 1], blocks[:, 0])
    got = lax.ppermute(give, "zl", [(0, 1), (1, 0)])
    strips, blocks, got = lax.optimization_barrier((strips, blocks, got))
    terms = jnp.where(zl == 0, blocks[:, 0], blocks[:, 1]).astype(F32) + got.astype(F32)
    terms = terms.astype(BF16).reshape(Z // 2 * rows, 2 * rows)

    def place(k):
        pairs = [(cs * X + xs, (xs // 2) * X + 2 * cs + ((xs % 2) ^ k)) for cs in range(C) for xs in range(X)]
        block = jnp.where((x % 2) ^ k == 0, terms[:, :rows], terms[:, rows:])
        return lax.ppermute(block, ("c", "x"), pairs).reshape(Z // 2, rows, rows)

    near, far = place(0), place(1)
    terms = jnp.concatenate([jnp.where(even, near, far), jnp.where(even, far, near)], axis=1)

    (top,) = in_vmem(first_rows, [(Z * C, strip_rows, 9 * rows)], (SUB, LANES), "first_rows", strips)
    top = lax.all_to_all(top, GROUP, 0, 0, tiled=True).reshape(rows, 9 * rows)
    top, terms = lax.optimization_barrier((top, terms))
    top_cols = jnp.concatenate([top[:, rows:4 * rows], top[:, 6 * rows:]], axis=0)
    update = jnp.sum(lax.all_to_all(terms, "zh", 0, 0, tiled=True).astype(F32), axis=0)

    (inverse,) = in_vmem(inverse_factor, [(width, width)], (width, 2 * width), "inverse_factor", top[:, :rows], top[:, 4 * rows:6 * rows])
    inverse, update = lax.optimization_barrier((inverse, update))
    level = jnp.dot(inverse, top_cols, precision=HI).astype(BF16)
    level_own = level[:, :rows]
    level_rows = level[:, rows:]

    outer = lax.dot_general(
        level_rows, level_own, (((0,), (0,)), ((), ())), preferred_element_type=F32
    )
    keep = ((z > 0) | (c > 0)) & ((y > 0) | (x > 1))
    schur_next = jnp.where(keep, (separator - update) - outer, jnp.float32(0.0))
    return (panels, level_own, schur_next)


def solution(mesh):
    fine = Mesh(mesh.devices.reshape(Z // 2, 2, C, Y, X), GROUP + ("y", "x"))
    grp, rd = GROUP, ("y", "x")
    return jax.shard_map(
        body,
        mesh=fine,
        in_specs=(
            P(grp, rd, None),
            P(grp, None, None),
            P(grp, None),
            P(grp),
            P(grp, rd),
        ),
        out_specs=(P(grp, rd, None), P(None, rd), P(grp, rd)),
        check_vma=False,
    )
```
